128 devices in a mesh: prow: 8 (over z, core), pcol: 16 (over y, x).
Axes of the slice: x: 4, y: 4, z: 4, core: 2. Of those that a mesh axis runs over, the one named last changes fastest.
Arguments:
- ancestor_inv: float32 [16384, 16384], P('prow', 'pcol'), as said below
- lhat_parent: float32 [16384, 512], P('pcol'), may hold values from -0.09375 to 0.09375
- lhat_child: float32 [16384, 512], P('pcol'), may hold values from -0.09375 to 0.09375
- lhat_cross: float32 [512, 512], replicated, may hold values from -0.25 to 0.25
- diag_parent: float32 [512, 512], replicated, as said below
- diag_child: float32 [512, 512], replicated, as said below
- structure: int32 [2, 64], replicated, may hold values from 0 to 1, as said below
- widths: int32 [2], replicated, may hold values from 64 to 512, as said below
Outputs:
- inv_sp: float32 [16384, 512], P('pcol')
- inv_pp: float32 [512, 512], replicated
- inv_sc: float32 [16384, 512], P('pcol')
- inv_pc: float32 [512, 512], replicated
- inv_cc: float32 [512, 512], replicated
The draws below stay inside these ranges and needn't reach their ends.
Inputs may be any that keep to these rules, and one draw needn't show every extreme that they name: ancestor_inv is exactly symmetric: the identity plus a symmetric part whose entries are of order 1 / sqrt(16384). diag_parent is exactly symmetric: 1.5 times the identity plus a symmetric part whose entries are of order 1 / sqrt(512). diag_child is exactly symmetric: 1.5 times the identity plus a symmetric part whose entries are of order 1 / sqrt(512). `structure`: 0 or 1; every block in the child's structure is in the parent's. `widths`: one of the two equals 512.
All inputs are finite; a program needn't handle non-finite values.
Results may differ from the reference program's by a relative error of at most 0.000073.
Values sent between devices are 32-bit elements; how exact they have to be, the bound alone decides.
No kernel may reach another device: no remote copies, remote signals or barrier semaphores. Data moves between devices by JAX's collectives and lax.ppermute only.
A program may use at most 128 MiB of HBM per device.

```python
import jax
import jax.numpy as jnp
from jax import lax

W = 512
BLK = 256
NS = 16384
NBLK = 64


def symmetric_block(key, order, diagonal):
    raw = jax.random.normal(key, (order, order), jnp.float32)
    return (raw + raw.T) * (0.5 / order ** 0.5) + diagonal * jnp.eye(order, dtype=jnp.float32)


def draw_ancestor_inv(key, part):
    key = jax.random.fold_in(key, 11)
    return symmetric_block(key, NS, 1.0)


def draw_diag_parent(key, part):
    key = jax.random.fold_in(key, 12)
    return symmetric_block(key, W, 1.5)


def draw_diag_child(key, part):
    key = jax.random.fold_in(key, 13)
    return symmetric_block(key, W, 1.5)


def draw_structure(key, part):
    key = jax.random.fold_in(key, 14)
    first, second = jax.random.split(key)
    parent = (jax.random.randint(first, (NBLK,), 0, 5) < 3).astype(jnp.int32)
    child = parent * (jax.random.randint(second, (NBLK,), 0, 5) < 3).astype(jnp.int32)
    return jnp.stack([parent, child])


def draw_widths(key, part):
    key = jax.random.fold_in(key, 15)
    first, second = jax.random.split(key)
    drawn = jax.random.randint(first, (2,), W // 8, W + 1)
    which = jax.random.randint(second, (), 0, 2)
    return jnp.where(jnp.arange(2, dtype=jnp.int32) == which, W, drawn).astype(jnp.int32)


def steps_of(rng, shape, shards, smallest, high):
    def one(dim, blocks):
        heights = jax.random.uniform(jax.random.fold_in(jax.random.fold_in(rng, 6), dim), (blocks,), jnp.float32, smallest / len(shards), high / len(shards))
        return jnp.repeat(jnp.exp(heights), shape[dim] // blocks).reshape((-1,) + (1,) * (len(shape) - dim - 1))

    gain = one(*shards[0])
    for cut in shards[1:]:
        gain = gain * one(*cut)
    return gain


def bell_draw(key, dims, scale, limit, cuts=(), held_as=jnp.bfloat16):
    values = jax.random.normal(key, dims, jnp.float32) * scale
    if len(cuts) > 0:
        values = steps_of(key, dims, cuts, -0.22, 0.18) * values
    return jnp.clip(values, min=-limit, max=limit).astype(held_as)


def setup_inputs(seed: int = 0) -> dict:
    splits = jax.random.split(jax.random.key(seed), 9)
    ancestor_inv = draw_ancestor_inv(jax.random.fold_in(splits[8], 71), 0)
    lhat_parent = bell_draw(splits[1], (NS, W), (NS // 4) ** -0.5, 0.09375, ((0, 16),), jnp.float32)
    lhat_child = bell_draw(splits[2], (NS, W), (NS // 4) ** -0.5, 0.09375, ((0, 16),), jnp.float32)
    lhat_cross = bell_draw(splits[3], (W, W), W ** -0.5, 0.25, (), jnp.float32)
    diag_parent = draw_diag_parent(jax.random.fold_in(splits[8], 71), 0)
    diag_child = draw_diag_child(jax.random.fold_in(splits[8], 71), 0)
    structure = draw_structure(jax.random.fold_in(splits[8], 71), 0)
    widths = draw_widths(jax.random.fold_in(splits[8], 71), 0)
    return dict(ancestor_inv=ancestor_inv, lhat_parent=lhat_parent, lhat_child=lhat_child, lhat_cross=lhat_cross, diag_parent=diag_parent, diag_child=diag_child, structure=structure, widths=widths)


def matmul(left, right):
    return jnp.dot(left, right, precision=lax.Precision.HIGHEST, preferred_element_type=jnp.float32)


def inner(left, right):
    return lax.dot_general(left, right, (((0,), (0,)), ((), ())), precision=lax.Precision.HIGHEST, preferred_element_type=jnp.float32)


def reference(ancestor_inv, lhat_parent, lhat_child, lhat_cross, diag_parent, diag_child, structure, widths):
    rmask = jnp.repeat(structure.astype(jnp.float32), BLK, axis=1)
    cmask = (jnp.arange(W, dtype=jnp.int32)[None, :] < widths[:, None]).astype(jnp.float32)
    lp = lhat_parent * rmask[0][:, None] * cmask[0][None, :]
    lc = lhat_child * rmask[1][:, None] * cmask[1][None, :]
    cross = lhat_cross * cmask[0][:, None] * cmask[1][None, :]
    dp = diag_parent * cmask[0][:, None] * cmask[0][None, :]
    dc = diag_child * cmask[1][:, None] * cmask[1][None, :]
    inv_sp = -matmul(ancestor_inv, lp) * rmask[0][:, None]
    inv_pp = dp - inner(lp, inv_sp)
    inv_pc = -(matmul(inv_pp, cross) + inner(inv_sp, lc))
    inv_sc = -(matmul(ancestor_inv, lc) + matmul(inv_sp, cross)) * rmask[1][:, None]
    inv_cc = dc - inner(cross, inv_pc) - inner(lc, inv_sc)
    return inv_sp, inv_pp, inv_sc, inv_pc, inv_cc
```

```python
import jax
import jax.numpy as jnp
from jax import lax
from jax.experimental import pallas as pl
from jax.experimental.pallas import tpu as pltpu
from jax.sharding import PartitionSpec as P

BLK = 256
AXES = ("prow", "pcol")
SIDE = 4
LANES = 128
MIB = 1 << 20
SPAN = range(SIDE)
CHUNKS = 2 * SIDE
SLICE = 16
CAPACITIES = ((30, 24), (36, 26), (42, 28), (50, 32), (64, 32))
BUCKET, FIRST_COUNT, SECOND_COUNT, SLICE_A, SLICE_B, TURNED, PLANE_Z, CORE, OUTER = range(9)
OWN, ROW, WIDTHS, PLAN_SIZE = 16, 48, 112, 128


def flat(z, k, y, x):
    return ((z % SIDE) * 2 + k) * SIDE * SIDE + (y % SIDE) * SIDE + x % SIDE


PLACES = [(z, k, y, x) for z in SPAN for k in (0, 1) for y in SPAN for x in SPAN]
ROWS_OF_CORE_0 = [[flat(z, 0, y, x) for x in SPAN] for z in SPAN for y in SPAN]
COLS_OF_CORE_0 = [[flat(z, 0, y, x) for y in SPAN] for z in SPAN for x in SPAN]
ROWS_OF_CORE_1 = [[flat(z, 1, y, x) for x in SPAN] for z in SPAN for y in SPAN]
COLS_OF_CORE_1 = [[flat(z, 1, y, x) for y in SPAN] for z in SPAN for x in SPAN]
NEAR = ROWS_OF_CORE_0 + COLS_OF_CORE_1
FAR = COLS_OF_CORE_0 + ROWS_OF_CORE_1
PLANE = [[flat(z, 0, y, x) for y in SPAN for x in SPAN] for z in SPAN] + [
    [flat(z, 1, y, x) for x in SPAN for y in SPAN] for z in SPAN
]
STACK = [[flat(z, k, y, x) for z in SPAN] for k in (0, 1) for y in SPAN for x in SPAN]


def piece_of(k, y, x):
    return SIDE * y + x if k == 0 else SIDE * x + y


def deals():
    pairs, slices, turned, used = [[], []], [[0] * 128, [0] * 128], [0] * 128, {}
    for z, k, y, x in PLACES:
        here, p = flat(z, k, y, x), piece_of(k, y, x)
        near = ((x - y) // 2) % 2
        turned[here] = near
        for i, block in enumerate((near, 1 - near)):
            plane = (z + x + y + 2 * k) % SIDE
            core = used.get((i, z, k, block, plane), 0)
            used[i, z, k, block, plane] = core + 1
            there = flat(plane, core, z, 2 * k + block)
            pairs[i].append((there, here))
            slices[i][there] = p
    return pairs, slices + [turned]


DEALS, DEAL_TABLE = deals()


def fetch_z(value, dz):
    pairs = [(flat(z + dz, k, y, x), flat(z, k, y, x)) for z, k, y, x in PLACES]
    return lax.ppermute(value, AXES, pairs)


def fetch_far(value, d):
    pairs = [(flat(z, k, y + d * (1 - k), x + d * k), flat(z, k, y, x)) for z, k, y, x in PLACES]
    return lax.ppermute(value, AXES, pairs)


def swap_cores(value):
    pairs = [(flat(z, 1 - k, y, x), flat(z, k, y, x)) for z, k, y, x in PLACES]
    return lax.ppermute(value, AXES, pairs)


def exchange(value, groups):
    return lax.all_to_all(value, AXES, 0, 0, axis_index_groups=groups, tiled=True)


def gather(value, groups):
    size = len(groups[0])
    return exchange(jnp.broadcast_to(value[None], (size,) + value.shape), groups)


def scatter_sum(value, groups):
    return jnp.sum(exchange(value, groups), axis=0)


def inner(left, right):
    return lax.dot_general(
        left, right, (((0,), (0,)), ((), ())), precision=lax.Precision.HIGH, preferred_element_type=jnp.float32
    )


def split(value):
    high = value.astype(jnp.bfloat16)
    return high, (value - high.astype(jnp.float32)).astype(jnp.bfloat16)


def dot3(left, right, dims=(((1,), (0,)), ((), ()))):
    left_high, left_low = split(left)
    right_high, right_low = split(right)

    def dot(a, b):
        return lax.dot_general(a, b, dims, preferred_element_type=jnp.float32)

    return dot(left_high, right_high) + (dot(left_high, right_low) + dot(left_low, right_high))


def split_transposed_kernel(a_ref, high_ref, low_ref):
    high, low = split(a_ref[...])
    high_ref[...] = high.T
    low_ref[...] = low.T


def split_transposed(a):
    rows, cols = a.shape
    return pl.pallas_call(
        split_transposed_kernel,
        grid=(rows // 256,),
        in_specs=[pl.BlockSpec((256, cols), lambda i: (i, 0))],
        out_specs=[pl.BlockSpec((cols, 256), lambda i: (0, i))] * 2,
        out_shape=[jax.ShapeDtypeStruct((cols, rows), jnp.bfloat16)] * 2,
        compiler_params=pltpu.CompilerParams(vmem_limit_bytes=16 * MIB),
        cost_estimate=pl.CostEstimate(flops=rows * cols, bytes_accessed=8 * rows * cols, transcendentals=0),
    )(a)


def smem(*shape):
    return pl.BlockSpec(memory_space=pltpu.SMEM)


def plan_kernel(place_ref, structure_ref, widths_ref, table_ref, plan_ref, counts):
    r, c = place_ref[0], place_ref[1]
    chunks = [(widths_ref[i] + LANES - 1) // LANES for i in range(2)]

    def zero(i, _):
        plan_ref[i] = 0
        return 0

    lax.fori_loop(0, PLAN_SIZE, zero, 0)

    def count(col, most):
        total = jnp.int32(0)
        for b in range(4):
            for i in range(2):
                total += jnp.where(structure_ref[i, 4 * col + b] > 0, chunks[i], 0)
        counts[col] = total
        return jnp.maximum(most, total)

    most_col = lax.fori_loop(0, 16, count, jnp.int32(0))
    most_row = lax.fori_loop(0, 8, lambda i, m: jnp.maximum(m, counts[2 * i] + counts[2 * i + 1]), jnp.int32(0))
    bucket = jnp.int32(0)
    for row_slots, col_slots in CAPACITIES[:-1]:
        bucket += jnp.where((most_row > row_slots) | (most_col > col_slots), 1, 0)
    plan_ref[BUCKET] = bucket

    def mark(start, base, blocks):
        def one(b, run):
            for q in range(CHUNKS):
                active = (structure_ref[q // SIDE, start + b] > 0) & (q % SIDE < chunks[q // SIDE])
                plan_ref[base + b * CHUNKS + q] = jnp.where(active, run, -1)
                run += jnp.where(active, 1, 0)
            return run

        return lax.fori_loop(0, blocks, one, jnp.int32(0))

    mark(4 * c, OWN, 4)
    mark(8 * r, ROW, 8)
    plan_ref[FIRST_COUNT] = counts[2 * r]
    plan_ref[SECOND_COUNT] = counts[2 * r + 1]
    here = r * 16 + c
    plan_ref[SLICE_A] = table_ref[0, here]
    plan_ref[SLICE_B] = table_ref[1, here]
    plan_ref[TURNED] = table_ref[2, here]
    plan_ref[PLANE_Z] = r // 2
    core = lax.rem(r, 2)
    plan_ref[CORE] = core
    plan_ref[OUTER] = jnp.where(core == 0, c // SIDE, lax.rem(c, SIDE))
    for i in range(2):
        plan_ref[WIDTHS + i] = widths_ref[i]


def make_plan(place, structure, widths):
    return pl.pallas_call(
        plan_kernel,
        in_specs=[smem()] * 4,
        out_specs=smem(),
        out_shape=jax.ShapeDtypeStruct((PLAN_SIZE,), jnp.int32),
        scratch_shapes=[pltpu.SMEM((16,), jnp.int32)],
    )(place, structure, widths, jnp.array(DEAL_TABLE, jnp.int32))


def pack_kernel(plan_ref, parent_a, parent_b, child_a, child_b, out_a, out_b):
    lane = lax.broadcasted_iota(jnp.int32, (SLICE, LANES), 1)
    for q in range(CHUNKS):
        panels = ((parent_a, parent_b), (child_a, child_b))[q // SIDE]
        cols = pl.ds(LANES * (q % SIDE), LANES)
        mask = jnp.where(lane + LANES * (q % SIDE) < plan_ref[WIDTHS + q // SIDE], 1.0, 0.0)
        for b in range(4):
            slot = plan_ref[OWN + b * CHUNKS + q]

            @pl.when(slot >= 0)
            def _():
                for panel, out in zip(panels, (out_a, out_b)):
                    out[slot] = panel[b, :, cols] * mask


def pack(plan, parent, child, slots):
    width = parent.shape[1]
    shaped = [panel.reshape(4, BLK, width) for panel in (parent, child)]
    specs = [pl.BlockSpec((4, SLICE, width), lambda i, plan, at=at: (0, plan[at], 0)) for at in (SLICE_A, SLICE_B)]
    out = pl.BlockSpec((slots, SLICE, LANES), lambda i, plan: (0, 0, 0))
    return pl.pallas_call(
        pack_kernel,
        grid_spec=pltpu.PrefetchScalarGridSpec(
            num_scalar_prefetch=1, grid=(1,), in_specs=specs + specs, out_specs=[out, out]
        ),
        out_shape=[jax.ShapeDtypeStruct((slots, SLICE, LANES), jnp.float32)] * 2,
        compiler_params=pltpu.CompilerParams(vmem_limit_bytes=16 * MIB),
        cost_estimate=pl.CostEstimate(flops=0, bytes_accessed=4 * MIB, transcendentals=0),
    )(plan, shaped[0], shaped[0], shaped[1], shaped[1])


def merge_kernel(plan_ref, from_a, from_b, out_ref):
    turned = plan_ref[TURNED] > 0
    first, second = plan_ref[FIRST_COUNT], plan_ref[SECOND_COUNT]

    def copy(source, count, start):
        def one(e, _):
            value = source[e]
            for i in SPAN:
                out_ref[i, start + e] = value
            return 0

        lax.fori_loop(0, count, one, 0)

    @pl.when(turned)
    def _():
        copy(from_b, first, 0)
        copy(from_a, second, first)

    @pl.when(jnp.logical_not(turned))
    def _():
        copy(from_a, first, 0)
        copy(from_b, second, first)


def merge(plan, from_a, from_b, slots):
    ins = pl.BlockSpec(from_a.shape, lambda i, plan: (0, 0, 0))
    return pl.pallas_call(
        merge_kernel,
        grid_spec=pltpu.PrefetchScalarGridSpec(
            num_scalar_prefetch=1,
            grid=(1,),
            in_specs=[ins, ins],
            out_specs=pl.BlockSpec((SIDE, slots, SLICE, LANES), lambda i, plan: (0, 0, 0, 0)),
        ),
        out_shape=jax.ShapeDtypeStruct((SIDE, slots, SLICE, LANES), jnp.float32),
        compiler_params=pltpu.CompilerParams(vmem_limit_bytes=16 * MIB),
        cost_estimate=pl.CostEstimate(flops=0, bytes_accessed=4 * MIB, transcendentals=0),
    )(plan, from_a, from_b)


def product_kernel(plan_ref, high_ref, low_ref, *refs):
    pieces, (mine_ref, send_ref, panel_high, panel_low, total) = refs[:5], refs[5:]
    own, ahead, behind, far_first, far_last = pieces
    step = pl.program_id(0)
    outer = plan_ref[OUTER]

    @pl.when(step == 0)
    def _():
        total[...] = jnp.zeros_like(total)

    for i in range(2):
        slots = [plan_ref[ROW + step * CHUNKS + SIDE * i + q] for q in SPAN]

        @pl.when(slots[0] >= 0)
        def _():
            for q in SPAN:
                cols = pl.ds(LANES * q, LANES)

                @pl.when(slots[q] >= 0)
                def _():
                    for ref, d, inner_start in (
                        (own, 0, 0), (ahead, 1, 0), (far_first, 2, 0), (far_last, 2, 2), (behind, 3, 0)
                    ):
                        count = ref.shape[0] * SLICE
                        start = SIDE * SLICE * lax.rem(outer + d, SIDE) + SLICE * inner_start
                        rows = pl.ds(pl.multiple_of(start, 2 * SLICE), count)
                        high, low = split(ref[:, slots[q]].reshape(count, LANES))
                        panel_high[rows, cols] = high
                        panel_low[rows, cols] = low

                @pl.when(slots[q] < 0)
                def _():
                    panel_high[:, cols] = jnp.zeros((BLK, LANES), jnp.bfloat16)
                    panel_low[:, cols] = jnp.zeros((BLK, LANES), jnp.bfloat16)

            @pl.loop(0, high_ref.shape[0] // 512)
            def _(t):
                rows = pl.ds(pl.multiple_of(512 * t, 512), 512)
                part = jnp.dot(high_ref[rows, :], panel_high[...], preferred_element_type=jnp.float32)
                part += jnp.dot(high_ref[rows, :], panel_low[...], preferred_element_type=jnp.float32)
                part += jnp.dot(low_ref[rows, :], panel_high[...], preferred_element_type=jnp.float32)
                for q in SPAN:
                    total[SIDE * i + q, rows, :] += part[:, LANES * q : LANES * (q + 1)]

    @pl.when(step == pl.num_programs(0) - 1)
    def _():
        for q in range(CHUNKS):
            z, owner = 2 * (q // SIDE) + q % 2, (q % SIDE) // 2

            @pl.when(plan_ref[CORE] == owner)
            def _():
                mine_ref[z] = total[q]

            @pl.when(plan_ref[CORE] != owner)
            def _():
                send_ref[z] = total[q]


def product(plan, high, low, pieces):
    cols, rows = high.shape
    width = SIDE * LANES
    out = pl.BlockSpec((SIDE, cols, LANES), lambda i, plan: (0, 0, 0))
    return pl.pallas_call(
        product_kernel,
        grid_spec=pltpu.PrefetchScalarGridSpec(
            num_scalar_prefetch=1,
            grid=(rows // BLK,),
            in_specs=[pl.BlockSpec((cols, BLK), lambda i, plan: (0, i))] * 2
            + [pl.BlockSpec(piece.shape, lambda i, plan: (0, 0, 0, 0)) for piece in pieces],
            out_specs=[out, out],
            scratch_shapes=[pltpu.VMEM((BLK, width), jnp.bfloat16)] * 2
            + [pltpu.VMEM((CHUNKS, cols, LANES), jnp.float32)],
        ),
        out_shape=[jax.ShapeDtypeStruct((SIDE, cols, LANES), jnp.float32)] * 2,
        compiler_params=pltpu.CompilerParams(vmem_limit_bytes=48 * MIB),
        cost_estimate=pl.CostEstimate(
            flops=6 * rows * cols * width, bytes_accessed=16 * rows * cols, transcendentals=0
        ),
    )(plan, high, low, *pieces)


def products(row_slots, col_slots):
    def run(plan, ancestor_inv, parent, child):
        sent = pack(plan, parent, child, col_slots)
        dealt = [lax.ppermute(value, AXES, pairs) for value, pairs in zip(sent, DEALS)]
        high, low = split_transposed(ancestor_inv)
        near = exchange(merge(plan, *dealt, row_slots), NEAR)
        ahead, behind = fetch_far(near, 1), fetch_far(near, 3)
        far_first, far_last = fetch_far(ahead[:2], 1), fetch_far(behind[2:], 3)
        return product(plan, high, low, (near, ahead, behind, far_first, far_last))

    return run


def slab_chunk(z, k):
    return SIDE * (z // 2) + 2 * k + lax.rem(z, 2)


def masked_cross(plan_ref, cross_ref):
    rows = lax.broadcasted_iota(jnp.int32, cross_ref.shape, 0)
    cols = lax.broadcasted_iota(jnp.int32, cross_ref.shape, 1)
    keep = jnp.where(rows < plan_ref[WIDTHS], 1.0, 0.0) * jnp.where(cols < plan_ref[WIDTHS + 1], 1.0, 0.0)
    return cross_ref[...] * keep


def masked_square(ref, width):
    rows = lax.broadcasted_iota(jnp.int32, ref.shape, 0)
    cols = lax.broadcasted_iota(jnp.int32, ref.shape, 1)
    return ref[...] * (jnp.where(rows < width, 1.0, 0.0) * jnp.where(cols < width, 1.0, 0.0))


def rows_kernel(plan_ref, own_ref, other_ref, cross_ref, inv_sp_ref, inv_sc_ref, total):
    z, k = plan_ref[PLANE_Z], plan_ref[CORE]
    for ref, core in ((own_ref, k), (other_ref, 1 - k)):
        for d in SPAN:
            start = LANES * slab_chunk(lax.rem(z + d, SIDE), core)
            total[:, pl.ds(pl.multiple_of(start, LANES), LANES)] = ref[d]
    width = cross_ref.shape[0]
    block = OWN + pl.program_id(0) * CHUNKS
    keep = [jnp.where(plan_ref[block + SIDE * i] >= 0, 1.0, 0.0) for i in range(2)]
    inv_sp = -total[:, :width] * keep[0]
    inv_sp_ref[...] = inv_sp
    inv_sc_ref[...] = -(total[:, width:] + dot3(inv_sp, masked_cross(plan_ref, cross_ref))) * keep[1]


def finish_rows(plan, own, other, cross):
    _, rows, _ = own.shape
    width = cross.shape[0]
    slabs = pl.BlockSpec((SIDE, BLK, LANES), lambda i, plan: (0, i, 0))
    whole = pl.BlockSpec((BLK, width), lambda i, plan: (i, 0))
    return pl.pallas_call(
        rows_kernel,
        grid_spec=pltpu.PrefetchScalarGridSpec(
            num_scalar_prefetch=1,
            grid=(rows // BLK,),
            in_specs=[slabs, slabs, pl.BlockSpec((width, width), lambda i, plan: (0, 0))],
            out_specs=[whole, whole],
            scratch_shapes=[pltpu.VMEM((BLK, 2 * width), jnp.float32)],
        ),
        out_shape=[jax.ShapeDtypeStruct((rows, width), jnp.float32)] * 2,
        compiler_params=pltpu.CompilerParams(vmem_limit_bytes=32 * MIB),
        cost_estimate=pl.CostEstimate(flops=6 * rows * width * width, bytes_accessed=16 * rows * width, transcendentals=0),
    )(plan, own, other, cross)


def blocks_kernel(plan_ref, own_ref, other_ref, cross_ref, parent_ref, child_ref, inv_pp_ref, inv_pc_ref, inv_cc_ref, slab, total):
    share = own_ref.shape[2]
    k = plan_ref[CORE]
    for ref, core in ((own_ref, k), (other_ref, 1 - k)):
        for z in SPAN:
            j = SIDE * (z // 2) + 2 * core + z % 2
            for p in range(16):
                slab[j, pl.ds(share * p, share), :] = ref[p, z]
    for j in range(CHUNKS):
        for i in range(CHUNKS):
            t = (i - j) % CHUNKS
            if t <= 4:
                block = slab[j, pl.ds(LANES * t, LANES), :]
            else:
                block = slab[i, pl.ds(LANES * (CHUNKS - t), LANES), :].T
            total[pl.ds(LANES * i, LANES), pl.ds(LANES * j, LANES)] = block
    width = cross_ref.shape[0]
    cross = masked_cross(plan_ref, cross_ref)
    inv_pp = masked_square(parent_ref, plan_ref[WIDTHS]) + total[:width, :width]
    inv_pp_ref[...] = inv_pp
    inv_pc = total[:width, width:] - dot3(inv_pp, cross)
    inv_pc_ref[...] = inv_pc
    last = dot3(cross, inv_pc, (((0,), (0,)), ((), ()))) + dot3(total[width:, :width], cross)
    inv_cc_ref[...] = masked_square(child_ref, plan_ref[WIDTHS + 1]) + total[width:, width:] - last


def finish_blocks(plan, own, other, cross, parent, child):
    width = cross.shape[0]
    square = pl.BlockSpec((width, width), lambda i, plan: (0, 0))
    sums = pl.BlockSpec(own.shape, lambda i, plan: (0, 0, 0, 0))
    return pl.pallas_call(
        blocks_kernel,
        grid_spec=pltpu.PrefetchScalarGridSpec(
            num_scalar_prefetch=1,
            grid=(1,),
            in_specs=[sums, sums, square, square, square],
            out_specs=[square] * 3,
            scratch_shapes=[
                pltpu.VMEM((CHUNKS, 5 * LANES, LANES), jnp.float32),
                pltpu.VMEM((2 * width, 2 * width), jnp.float32),
            ],
        ),
        out_shape=[jax.ShapeDtypeStruct((width, width), jnp.float32)] * 3,
        compiler_params=pltpu.CompilerParams(vmem_limit_bytes=32 * MIB),
        cost_estimate=pl.CostEstimate(flops=18 * width**3, bytes_accessed=40 * width * width, transcendentals=0),
    )(plan, own, other, cross, parent, child)


def per_device(
    ancestor_inv, lhat_parent, lhat_child, lhat_cross, diag_parent, diag_child, structure, widths
):
    c = lax.axis_index("pcol")
    r = lax.axis_index("prow")
    z, k = r // 2, lax.rem(r, 2)
    block_rows, width = lhat_parent.shape
    blocks_here = block_rows // BLK
    plan = make_plan(jnp.stack([r, c]).astype(jnp.int32), structure, widths)
    mine, send = lax.switch(
        plan[BUCKET], [products(*slots) for slots in CAPACITIES], plan, ancestor_inv, lhat_parent, lhat_child)
    slab = scatter_sum(mine + swap_cores(send), STACK)

    local_struct = lax.dynamic_slice_in_dim(structure, c * blocks_here, blocks_here, 1)
    row_mask = jnp.repeat(local_struct.astype(jnp.float32), BLK, axis=1).T
    col_mask = (jnp.arange(width, dtype=jnp.int32)[None, :] < widths[:, None]).astype(jnp.float32)
    masked = jnp.concatenate(
        [panel * row_mask[:, i : i + 1] for i, panel in enumerate((lhat_parent, lhat_child))], axis=1
    ) * col_mask.reshape(1, 2 * width)
    turned = lax.dynamic_slice_in_dim(
        jnp.concatenate([masked, masked[:, : 5 * LANES]], axis=1), slab_chunk(z, k) * LANES, 5 * LANES, 1)

    sums = scatter_sum(inner(turned, slab).reshape(16, -1, LANES), PLANE)
    sums = gather(sums, STACK)
    slab, sums = lax.optimization_barrier((slab, sums))
    slabs = jnp.stack([slab] + [fetch_z(slab, d) for d in (1, 2, 3)])
    other_slabs = swap_cores(slabs)
    sums = gather(gather(sums, NEAR), FAR).reshape(16, SIDE, -1, LANES)
    other_sums = swap_cores(sums)

    inv_sp, inv_sc = finish_rows(plan, slabs, other_slabs, lhat_cross)
    inv_pp, inv_pc, inv_cc = finish_blocks(plan, sums, other_sums, lhat_cross, diag_parent, diag_child)
    return (inv_sp, inv_pp, inv_sc, inv_pc, inv_cc)


def solution(mesh):
    return jax.shard_map(
        per_device,
        mesh=mesh,
        in_specs=(P("prow", "pcol"), P("pcol", None), P("pcol", None), P(), P(), P(), P(), P()),
        out_specs=(P("pcol", None), P(), P("pcol", None), P(), P()),
        check_vma=False,
    )
```

```python
import functools

import jax
import jax.numpy as jnp
from jax import lax
from jax.experimental import pallas as pl
from jax.experimental.pallas import tpu as pltpu
from jax.sharding import PartitionSpec as P

BLK = 256
AXES = ("prow", "pcol")
SIDE = 4
LANES = 128
MIB = 1 << 20
SPAN = range(SIDE)
CHUNKS = 2 * SIDE
SLICE = 16
GROUP = SIDE * SLICE
CAPACITIES = (36, 46, 64)
COLUMN_SLOTS = 4 * CHUNKS
BUCKET, FIRST_COUNT, SECOND_COUNT, SLICE_A, SLICE_B, TURNED, PLANE_Z, CORE, OUTER = range(9)
OWN, ROW, WIDTHS, DEST, PLAN_SIZE = 16, 48, 112, 114, 128


def flat(z, k, y, x):
    return ((z % SIDE) * 2 + k) * SIDE * SIDE + (y % SIDE) * SIDE + x % SIDE


PLACES = [(z, k, y, x) for z in SPAN for k in (0, 1) for y in SPAN for x in SPAN]
ROWS_OF_CORE_0 = [[flat(z, 0, y, x) for x in SPAN] for z in SPAN for y in SPAN]
COLS_OF_CORE_0 = [[flat(z, 0, y, x) for y in SPAN] for z in SPAN for x in SPAN]
ROWS_OF_CORE_1 = [[flat(z, 1, y, x) for x in SPAN] for z in SPAN for y in SPAN]
COLS_OF_CORE_1 = [[flat(z, 1, y, x) for y in SPAN] for z in SPAN for x in SPAN]
NEAR = ROWS_OF_CORE_0 + COLS_OF_CORE_1
FAR = COLS_OF_CORE_0 + ROWS_OF_CORE_1
STACK = [[flat(z, k, y, x) for z in SPAN] for k in (0, 1) for y in SPAN for x in SPAN]
STACK = [[flat(z, k, y, x) for z in SPAN] for k in (0, 1) for y in SPAN for x in SPAN]
PLANE = [[flat(z, 0, y, x) for y in SPAN for x in SPAN] for z in SPAN] + [
    [flat(z, 1, y, x) for x in SPAN for y in SPAN] for z in SPAN
]


def piece_of(k, y, x):
    return SIDE * y + x if k == 0 else SIDE * x + y


def deals():
    pairs, slices, turned, used = [[], []], [[0] * 128, [0] * 128], [0] * 128, {}
    for z, k, y, x in PLACES:
        here, p = flat(z, k, y, x), piece_of(k, y, x)
        near = ((x - y) // 2) % 2
        turned[here] = near
        for i, block in enumerate((near, 1 - near)):
            plane = (z + x + y + 2 * k) % SIDE
            core = used.get((i, z, k, block, plane), 0)
            used[i, z, k, block, plane] = core + 1
            there = flat(plane, core, z, 2 * k + block)
            pairs[i].append((there, here))
            slices[i][there] = p
    return pairs, slices + [turned]


DEALS, DEAL_TABLE = deals()


def partner(z, k, near):
    return z ^ (1 if (k == 0) == near else 3)


def swap_planes(value, near):
    pairs = [(flat(partner(z, k, near), k, y, x), flat(z, k, y, x)) for z, k, y, x in PLACES]
    return lax.ppermute(value, AXES, pairs)


PLANE_ORDER = ((0, 3, 1, 2), (0, 1, 3, 2))


def plane_at(z, core, place):
    return z ^ jnp.where(core == 0, PLANE_ORDER[0][place], PLANE_ORDER[1][place])


def fetch_far(value, d):
    pairs = [(flat(z, k, y + d * (1 - k), x + d * k), flat(z, k, y, x)) for z, k, y, x in PLACES]
    return lax.ppermute(value, AXES, pairs)


def swap_cores(value):
    pairs = [(flat(z, 1 - k, y, x), flat(z, k, y, x)) for z, k, y, x in PLACES]
    return lax.ppermute(value, AXES, pairs)


def exchange(value, groups):
    return lax.all_to_all(value, AXES, 0, 0, axis_index_groups=groups, tiled=True)


def gather(value, groups):
    size = len(groups[0])
    return exchange(jnp.broadcast_to(value[None], (size,) + value.shape), groups)


def scatter_sum(value, groups):
    return jnp.sum(exchange(value, groups), axis=0)


def split(value):
    high = value.astype(jnp.bfloat16)
    return high, (value - high.astype(jnp.float32)).astype(jnp.bfloat16)


def dot3(left, right, dims=(((1,), (0,)), ((), ()))):
    left_high, left_low = split(left)
    right_high, right_low = split(right)

    def dot(a, b):
        return lax.dot_general(a, b, dims, preferred_element_type=jnp.float32)

    return dot(left_high, right_high) + (dot(left_high, right_low) + dot(left_low, right_high))


def split_transposed_kernel(a_ref, out_ref):
    for o in SPAN:
        parts = [a_ref[BLK * i + GROUP * o : BLK * i + GROUP * (o + 1), :] for i in range(2)]
        high, low = split(jnp.concatenate(parts, axis=0))
        out_ref[o, 0] = high.T
        out_ref[o, 1] = low.T


def split_transposed(a):
    rows, cols = a.shape
    out = pl.BlockSpec((SIDE, 2, cols, 2 * GROUP), lambda i: (0, 0, 0, i))
    return pl.pallas_call(
        split_transposed_kernel,
        grid=(rows // (2 * BLK),),
        in_specs=[pl.BlockSpec((2 * BLK, cols), lambda i: (i, 0))],
        out_specs=out,
        out_shape=jax.ShapeDtypeStruct((SIDE, 2, cols, rows // SIDE), jnp.bfloat16),
        compiler_params=pltpu.CompilerParams(vmem_limit_bytes=24 * MIB),
        cost_estimate=pl.CostEstimate(flops=rows * cols, bytes_accessed=8 * rows * cols, transcendentals=0),
    )(a)


def smem(*shape):
    return pl.BlockSpec(memory_space=pltpu.SMEM)


def plan_kernel(place_ref, structure_ref, widths_ref, table_ref, plan_ref, counts):
    r, c = place_ref[0], place_ref[1]
    chunks = [(widths_ref[i] + LANES - 1) // LANES for i in range(2)]

    def zero(i, _):
        plan_ref[i] = 0
        return 0

    lax.fori_loop(0, PLAN_SIZE, zero, 0)

    def count(col, _):
        total = jnp.int32(0)
        for b in range(4):
            for i in range(2):
                total += jnp.where(structure_ref[i, 4 * col + b] > 0, chunks[i], 0)
        counts[col] = total
        return 0

    lax.fori_loop(0, 16, count, 0)
    most_row = lax.fori_loop(0, 8, lambda i, m: jnp.maximum(m, counts[2 * i] + counts[2 * i + 1]), jnp.int32(0))
    bucket = jnp.int32(0)
    for slots in CAPACITIES[:-1]:
        bucket += jnp.where(most_row > slots, 1, 0)
    plan_ref[BUCKET] = bucket

    def mark(start, base, blocks):
        def one(b, run):
            for q in range(CHUNKS):
                active = (structure_ref[q // SIDE, start + b] > 0) & (q % SIDE < chunks[q // SIDE])
                plan_ref[base + b * CHUNKS + q] = jnp.where(active, run, -1)
                run += jnp.where(active, 1, 0)
            return run

        return lax.fori_loop(0, blocks, one, jnp.int32(0))

    mark(4 * c, OWN, 4)
    mark(8 * r, ROW, 8)
    plan_ref[FIRST_COUNT] = counts[2 * r]
    plan_ref[SECOND_COUNT] = counts[2 * r + 1]
    here = r * 16 + c
    plan_ref[SLICE_A] = table_ref[0, here]
    plan_ref[SLICE_B] = table_ref[1, here]
    plan_ref[TURNED] = table_ref[2, here]
    plan_ref[PLANE_Z] = r // 2
    core = lax.rem(r, 2)
    plan_ref[CORE] = core
    plan_ref[OUTER] = jnp.where(core == 0, c // SIDE, lax.rem(c, SIDE))
    for i in range(2):
        plan_ref[WIDTHS + i] = widths_ref[i]
    for q in range(CHUNKS):
        owner = (q % SIDE) // 2
        apart = (r // 2) ^ (2 * (q // SIDE) + q % 2)
        dest = jnp.int32(0)
        for n in range(1, SIDE):
            dest = jnp.where(apart == PLANE_ORDER[owner][n], n, dest)
        plan_ref[DEST + q] = dest + jnp.where(core == owner, 0, SIDE)


def make_plan(place, structure, widths):
    return pl.pallas_call(
        plan_kernel,
        in_specs=[smem()] * 4,
        out_specs=smem(),
        out_shape=jax.ShapeDtypeStruct((PLAN_SIZE,), jnp.int32),
        scratch_shapes=[pltpu.SMEM((16,), jnp.int32)],
    )(place, structure, widths, jnp.array(DEAL_TABLE, jnp.int32))


def pack_kernel(plan_ref, parent_a, parent_b, child_a, child_b, out_a, out_b):
    lane = lax.broadcasted_iota(jnp.int32, (SLICE, LANES), 1)
    for q in range(CHUNKS):
        panels = ((parent_a, parent_b), (child_a, child_b))[q // SIDE]
        cols = pl.ds(LANES * (q % SIDE), LANES)
        mask = jnp.where(lane + LANES * (q % SIDE) < plan_ref[WIDTHS + q // SIDE], 1.0, 0.0)
        for b in range(4):
            slot = plan_ref[OWN + b * CHUNKS + q]

            @pl.when(slot >= 0)
            def _():
                for panel, out in zip(panels, (out_a, out_b)):
                    out[slot] = panel[b, :, cols] * mask


def pack(plan, parent, child, slots):
    width = parent.shape[1]
    shaped = [panel.reshape(4, BLK, width) for panel in (parent, child)]
    specs = [pl.BlockSpec((4, SLICE, width), lambda i, plan, at=at: (0, plan[at], 0)) for at in (SLICE_A, SLICE_B)]
    out = pl.BlockSpec((slots, SLICE, LANES), lambda i, plan: (0, 0, 0))
    return pl.pallas_call(
        pack_kernel,
        grid_spec=pltpu.PrefetchScalarGridSpec(
            num_scalar_prefetch=1, grid=(1,), in_specs=specs + specs, out_specs=[out, out]
        ),
        out_shape=[jax.ShapeDtypeStruct((slots, SLICE, LANES), jnp.float32)] * 2,
        compiler_params=pltpu.CompilerParams(vmem_limit_bytes=60 * MIB),
        cost_estimate=pl.CostEstimate(flops=0, bytes_accessed=4 * MIB, transcendentals=0),
    )(plan, shaped[0], shaped[0], shaped[1], shaped[1])


def merge_kernel(plan_ref, from_a, from_b, out_ref):
    turned = plan_ref[TURNED] > 0
    first, second = plan_ref[FIRST_COUNT], plan_ref[SECOND_COUNT]

    def copy(source, count, start):
        def one(e, _):
            value = source[e]
            for i in SPAN:
                out_ref[i, start + e] = value
            return 0

        lax.fori_loop(0, count, one, 0)

    @pl.when(turned)
    def _():
        copy(from_b, first, 0)
        copy(from_a, second, first)

    @pl.when(jnp.logical_not(turned))
    def _():
        copy(from_a, first, 0)
        copy(from_b, second, first)


def merge(plan, from_a, from_b, slots):
    ins = pl.BlockSpec(from_a.shape, lambda i, plan: (0, 0, 0))
    return pl.pallas_call(
        merge_kernel,
        grid_spec=pltpu.PrefetchScalarGridSpec(
            num_scalar_prefetch=1,
            grid=(1,),
            in_specs=[ins, ins],
            out_specs=pl.BlockSpec((SIDE, slots, SLICE, LANES), lambda i, plan: (0, 0, 0, 0)),
        ),
        out_shape=jax.ShapeDtypeStruct((SIDE, slots, SLICE, LANES), jnp.float32),
        compiler_params=pltpu.CompilerParams(vmem_limit_bytes=16 * MIB),
        cost_estimate=pl.CostEstimate(flops=0, bytes_accessed=4 * MIB, transcendentals=0),
    )(plan, from_a, from_b)


def product_kernel(sizes, has_earlier, plan_ref, *refs):
    count = len(sizes)
    tiles, refs = refs[:count], refs[count:]
    pieces, refs = refs[: sum(sizes)], refs[sum(sizes) :]
    out_refs, (panel_high, panel_low) = refs[has_earlier:-2], refs[-2:]
    tile, depth = tiles[0].shape[2:]

    @pl.when(pl.program_id(0) == 0)
    def _():
        @pl.loop(0, depth // GROUP)
        def _(b):
            for q in range(CHUNKS):
                slot = plan_ref[ROW + b * CHUNKS + q]
                kept, slot = slot >= 0, jnp.maximum(slot, 0)
                cols = pl.ds(pl.multiple_of(LANES * plan_ref[DEST + q], LANES), LANES)
                first = 0
                for g, size in enumerate(sizes):
                    values = [ref[:, slot].reshape(-1, LANES) for ref in pieces[first : first + size]]
                    first += size
                    value = values[0] if size == 1 else jnp.concatenate(values, axis=0)
                    high, low = split(jnp.where(kept, value, 0.0))
                    rows = pl.ds(pl.multiple_of(GROUP * b + depth * g, GROUP), GROUP)
                    panel_high[rows, cols] = high
                    panel_low[rows, cols] = low

    width = SIDE * LANES

    def half(i):
        cols = pl.ds(width * i, width) if isinstance(i, int) else pl.ds(pl.multiple_of(width * i, width), width)
        total = None
        for g in range(count):
            rows = pl.ds(depth * g, depth)
            both = tiles[g][0].reshape(2 * tile, depth)
            part = jnp.dot(both, panel_high[rows, cols], preferred_element_type=jnp.float32)
            part = part[:tile] + part[tile:]
            part += jnp.dot(tiles[g][0, 0], panel_low[rows, cols], preferred_element_type=jnp.float32)
            total = part if total is None else total + part
        return [total[:, LANES * q : LANES * (q + 1)] for q in SPAN]

    if len(out_refs) == 1:

        @pl.loop(0, 2)
        def _(i):
            for q, value in enumerate(half(i)):
                out_refs[0][SIDE * i + q] = value + refs[0][SIDE * i + q] if has_earlier else value
    else:
        for i in range(2):
            for q, value in enumerate(half(i)):
                out_refs[2 * i + q // 2][q % 2] = value + refs[0][SIDE * i + q]


def product(plan, split_tile, shifts, groups, earlier=None, is_last=False):
    _, _, cols, depth = split_tile.shape
    tile = 256
    pieces = [piece for group in groups for piece in group]
    whole = pl.BlockSpec((CHUNKS, tile, LANES), lambda i, plan: (0, i, 0))
    pair = pl.BlockSpec((2, tile, LANES), lambda i, plan: (0, i, 0))
    tiles = [
        pl.BlockSpec(
            (1, 2, tile, depth), lambda i, plan, shift=shift: (lax.rem(plan[OUTER] + shift, SIDE), 0, i, 0))
        for shift in shifts
    ]
    kernel = functools.partial(product_kernel, [len(group) for group in groups], earlier is not None)
    return pl.pallas_call(
        kernel,
        grid_spec=pltpu.PrefetchScalarGridSpec(
            num_scalar_prefetch=1,
            grid=(cols // tile,),
            in_specs=tiles
            + [pl.BlockSpec(piece.shape, lambda i, plan: (0, 0, 0, 0)) for piece in pieces]
            + [whole] * (earlier is not None),
            out_specs=[pair] * 4 if is_last else whole,
            scratch_shapes=[pltpu.VMEM((depth * len(shifts), CHUNKS * LANES), jnp.bfloat16)] * 2,
        ),
        out_shape=[jax.ShapeDtypeStruct((2, cols, LANES), jnp.float32)] * 4
        if is_last
        else jax.ShapeDtypeStruct((CHUNKS, cols, LANES), jnp.float32),
        compiler_params=pltpu.CompilerParams(vmem_limit_bytes=32 * MIB),
        cost_estimate=pl.CostEstimate(
            flops=6 * len(shifts) * depth * cols * CHUNKS * LANES, bytes_accessed=12 * MIB, transcendentals=0
        ),
    )(plan, *[split_tile] * len(shifts), *pieces, *([] if earlier is None else [earlier]))


def products(slots):
    def run(plan, split_tile, dealt):
        near = exchange(merge(plan, *dealt, slots), NEAR)
        ahead, behind = fetch_far(near, 1), fetch_far(near, 3)
        total = product(plan, split_tile, (0,), ((near,),))
        total, ahead, behind = lax.optimization_barrier((total, ahead, behind))
        far_first, far_last = fetch_far(ahead[:2], 1), fetch_far(behind[2:], 3)
        total = product(plan, split_tile, (1, 3), ((ahead,), (behind,)), total)
        return product(plan, split_tile, (2,), ((far_first, far_last),), total, True)

    return run


def turn_kernel(plan_ref, parent_ref, child_ref, high_ref, low_ref):
    first = slab_chunk(plan_ref[PLANE_Z], plan_ref[CORE])
    t = pl.program_id(0)
    q = lax.rem(first + t, CHUNKS)
    lane = lax.broadcasted_iota(jnp.int32, (BLK, LANES), 1)
    for panel, ref in enumerate((parent_ref, child_ref)):

        @pl.when(q // SIDE == panel)
        def _():
            start = LANES * lax.rem(q, SIDE)
            cols = pl.ds(pl.multiple_of(start, LANES), LANES)
            mask = jnp.where(lane + start < plan_ref[WIDTHS + panel], 1.0, 0.0)
            for b in range(4):
                keep = jnp.where(plan_ref[OWN + b * CHUNKS + SIDE * panel] >= 0, 1.0, 0.0)
                rows = pl.ds(BLK * b, BLK)
                high, low = split(ref[rows, cols] * mask * keep)
                high_ref[:, rows] = high.T
                low_ref[:, rows] = low.T


def turn(plan, parent, child):
    rows, width = parent.shape
    out = pl.BlockSpec((LANES, rows), lambda t, plan: (t, 0))
    panel = pl.BlockSpec((rows, width), lambda t, plan: (0, 0))
    return pl.pallas_call(
        turn_kernel,
        grid_spec=pltpu.PrefetchScalarGridSpec(
            num_scalar_prefetch=1, grid=(5,), in_specs=[panel, panel], out_specs=[out, out]
        ),
        out_shape=[jax.ShapeDtypeStruct((5 * LANES, rows), jnp.bfloat16)] * 2,
        compiler_params=pltpu.CompilerParams(vmem_limit_bytes=48 * MIB),
        cost_estimate=pl.CostEstimate(flops=MIB, bytes_accessed=8 * MIB, transcendentals=0),
    )(plan, parent, child)


def slab_kernel(kept_ref, passed_ref, high_ref, low_ref, slab_ref, sums_ref):
    slab = kept_ref[...] + passed_ref[...]
    slab_ref[...] = slab
    slab_high, slab_low = split(slab)
    total = jnp.dot(high_ref[...], slab_high, preferred_element_type=jnp.float32)
    total += jnp.dot(high_ref[...], slab_low, preferred_element_type=jnp.float32)
    sums_ref[...] = total + jnp.dot(low_ref[...], slab_high, preferred_element_type=jnp.float32)


def finish_slab(kept, passed, high, low):
    rows, width = kept.shape
    return pl.pallas_call(
        slab_kernel,
        out_shape=[
            jax.ShapeDtypeStruct((rows, width), jnp.float32),
            jax.ShapeDtypeStruct((high.shape[0], width), jnp.float32),
        ],
        compiler_params=pltpu.CompilerParams(vmem_limit_bytes=16 * MIB),
        cost_estimate=pl.CostEstimate(flops=6 * high.size * width, bytes_accessed=6 * MIB, transcendentals=0),
    )(kept, passed, high, low)


def slab_chunk(z, k):
    return SIDE * (z // 2) + 2 * k + lax.rem(z, 2)


def masked_cross(plan_ref, cross_ref):
    rows = lax.broadcasted_iota(jnp.int32, cross_ref.shape, 0)
    cols = lax.broadcasted_iota(jnp.int32, cross_ref.shape, 1)
    keep = jnp.where(rows < plan_ref[WIDTHS], 1.0, 0.0) * jnp.where(cols < plan_ref[WIDTHS + 1], 1.0, 0.0)
    return cross_ref[...] * keep


def masked_square(ref, width):
    rows = lax.broadcasted_iota(jnp.int32, ref.shape, 0)
    cols = lax.broadcasted_iota(jnp.int32, ref.shape, 1)
    return ref[...] * (jnp.where(rows < width, 1.0, 0.0) * jnp.where(cols < width, 1.0, 0.0))


def rows_kernel(plan_ref, own_a, own_b, other_a, other_b, cross_ref, inv_sp_ref, inv_sc_ref, total):
    z, k = plan_ref[PLANE_Z], plan_ref[CORE]
    for refs, core in (((own_a, own_b), k), ((other_a, other_b), 1 - k)):
        for i in SPAN:
            start = LANES * slab_chunk(plane_at(z, core, i), core)
            total[:, pl.ds(pl.multiple_of(start, LANES), LANES)] = refs[i // 2][i % 2]
    width = cross_ref.shape[0]
    block = OWN + pl.program_id(0) * CHUNKS
    keep = [jnp.where(plan_ref[block + SIDE * i] >= 0, 1.0, 0.0) for i in range(2)]
    inv_sp = -total[:, :width] * keep[0]
    inv_sp_ref[...] = inv_sp
    inv_sc_ref[...] = -(total[:, width:] + dot3(inv_sp, masked_cross(plan_ref, cross_ref))) * keep[1]


def finish_rows(plan, slabs, cross):
    _, rows, _ = slabs[0].shape
    width = cross.shape[0]
    pair = pl.BlockSpec((2, BLK, LANES), lambda i, plan: (0, i, 0))
    whole = pl.BlockSpec((BLK, width), lambda i, plan: (i, 0))
    return pl.pallas_call(
        rows_kernel,
        grid_spec=pltpu.PrefetchScalarGridSpec(
            num_scalar_prefetch=1,
            grid=(rows // BLK,),
            in_specs=[pair] * 4 + [pl.BlockSpec((width, width), lambda i, plan: (0, 0))],
            out_specs=[whole, whole],
            scratch_shapes=[pltpu.VMEM((BLK, 2 * width), jnp.float32)],
        ),
        out_shape=[jax.ShapeDtypeStruct((rows, width), jnp.float32)] * 2,
        compiler_params=pltpu.CompilerParams(vmem_limit_bytes=32 * MIB),
        cost_estimate=pl.CostEstimate(flops=6 * rows * width * width, bytes_accessed=16 * rows * width, transcendentals=0),
    )(plan, *slabs, cross)


def blocks_kernel(
    plan_ref, own_ref, other_ref, cross_ref, parent_ref, child_ref, inv_pp_ref, inv_pc_ref, inv_cc_ref, slab, total
):
    share = own_ref.shape[2]
    k = plan_ref[CORE]
    for ref, core in ((own_ref, k), (other_ref, 1 - k)):
        for z in SPAN:
            j = SIDE * (z // 2) + 2 * core + z % 2
            for i in SPAN:
                slab[j, pl.ds(share * i, share), :] = ref[i, z]
    for j in range(CHUNKS):
        for i in range(CHUNKS):
            t = (i - j) % CHUNKS
            if t <= 4:
                block = slab[j, pl.ds(LANES * t, LANES), :]
            else:
                block = slab[i, pl.ds(LANES * (CHUNKS - t), LANES), :].T
            total[pl.ds(LANES * i, LANES), pl.ds(LANES * j, LANES)] = block
    width = cross_ref.shape[0]
    cross = masked_cross(plan_ref, cross_ref)
    inv_pp = masked_square(parent_ref, plan_ref[WIDTHS]) + total[:width, :width]
    inv_pp_ref[...] = inv_pp
    inv_pc = total[:width, width:] - dot3(inv_pp, cross)
    inv_pc_ref[...] = inv_pc
    last = dot3(cross, inv_pc, (((0,), (0,)), ((), ()))) + dot3(total[width:, :width], cross)
    inv_cc_ref[...] = masked_square(child_ref, plan_ref[WIDTHS + 1]) + total[width:, width:] - last


def finish_blocks(plan, own, other, cross, parent, child):
    width = cross.shape[0]
    square = pl.BlockSpec((width, width), lambda i, plan: (0, 0))
    sums = pl.BlockSpec(own.shape, lambda i, plan: (0, 0, 0, 0))
    return pl.pallas_call(
        blocks_kernel,
        grid_spec=pltpu.PrefetchScalarGridSpec(
            num_scalar_prefetch=1,
            grid=(1,),
            in_specs=[sums, sums] + [square] * 3,
            out_specs=[square] * 3,
            scratch_shapes=[
                pltpu.VMEM((CHUNKS, 5 * LANES, LANES), jnp.float32),
                pltpu.VMEM((2 * width, 2 * width), jnp.float32),
            ],
        ),
        out_shape=[jax.ShapeDtypeStruct((width, width), jnp.float32)] * 3,
        compiler_params=pltpu.CompilerParams(vmem_limit_bytes=32 * MIB),
        cost_estimate=pl.CostEstimate(flops=18 * width**3, bytes_accessed=40 * width * width, transcendentals=0),
    )(plan, own, other, cross, parent, child)


def per_device(
    ancestor_inv, lhat_parent, lhat_child, lhat_cross, diag_parent, diag_child, structure, widths
):
    place = jnp.stack([lax.axis_index("prow"), lax.axis_index("pcol")]).astype(jnp.int32)
    plan = make_plan(place, structure, widths)
    sent = pack(plan, lhat_parent, lhat_child, COLUMN_SLOTS)
    dealt = [lax.ppermute(value, AXES, pairs) for value, pairs in zip(sent, DEALS)]
    split_tile, *dealt = lax.optimization_barrier((split_transposed(ancestor_inv), *dealt))
    kept, passed, send_kept, send_passed = lax.switch(
        plan[BUCKET], [products(slots) for slots in CAPACITIES], plan, split_tile, dealt)

    passed = swap_planes(passed + swap_cores(send_passed), True)
    kept = kept + swap_cores(send_kept)
    kept, passed, high, low = lax.optimization_barrier((kept, passed, *turn(plan, lhat_parent, lhat_child)))
    kept = kept + passed
    slab, sums = finish_slab(kept[0], swap_planes(kept[1], False), high, low)

    far_slab = swap_planes(slab, False)
    sums = scatter_sum(sums.reshape(SIDE, -1, LANES), NEAR)
    far_slab, sums = lax.optimization_barrier((far_slab, sums))
    first = jnp.stack([slab, far_slab])
    second, other_first = swap_planes(first, True), swap_cores(first)
    sums = jnp.sum(gather(sums, FAR), axis=0)
    sums = gather(sums, STACK)
    second, other_first, sums = lax.optimization_barrier((second, other_first, sums))
    other_second = swap_cores(second)
    sums = gather(sums, NEAR)
    other_second, sums = lax.optimization_barrier((other_second, sums))
    other_sums = swap_cores(sums)
    inv_sp, inv_sc = finish_rows(plan, (first, second, other_first, other_second), lhat_cross)
    inv_sp, inv_sc, other_sums = lax.optimization_barrier((inv_sp, inv_sc, other_sums))
    inv_pp, inv_pc, inv_cc = finish_blocks(plan, sums, other_sums, lhat_cross, diag_parent, diag_child)
    return (inv_sp, inv_pp, inv_sc, inv_pc, inv_cc)


def solution(mesh):
    return jax.shard_map(
        per_device,
        mesh=mesh,
        in_specs=(P("prow", "pcol"), P("pcol", None), P("pcol", None), P(), P(), P(), P(), P()),
        out_specs=(P("pcol", None), P(), P("pcol", None), P(), P()),
        check_vma=False,
    )
```

```python
import functools

import jax
import jax.numpy as jnp
from jax import lax
from jax.experimental import pallas as pl
from jax.experimental.pallas import tpu as pltpu
from jax.sharding import PartitionSpec as P

BLK = 256
AXES = ("prow", "pcol")
SIDE = 4
LANES = 128
MIB = 1 << 20
SPAN = range(SIDE)
CHUNKS = 2 * SIDE
SLICE = 16
GROUP = SIDE * SLICE
CAPACITIES = (36, 46, 64)
BUCKET, TURNED, PLANE_Z, CORE, OUTER = range(5)
OWN, ROW, WIDTHS, DEST, PLAN_SIZE = 16, 48, 112, 114, 128


def flat(z, k, y, x):
    return ((z % SIDE) * 2 + k) * SIDE * SIDE + (y % SIDE) * SIDE + x % SIDE


PLACES = [(z, k, y, x) for z in SPAN for k in (0, 1) for y in SPAN for x in SPAN]
ROWS_OF_CORE_0 = [[flat(z, 0, y, x) for x in SPAN] for z in SPAN for y in SPAN]
COLS_OF_CORE_0 = [[flat(z, 0, y, x) for y in SPAN] for z in SPAN for x in SPAN]
ROWS_OF_CORE_1 = [[flat(z, 1, y, x) for x in SPAN] for z in SPAN for y in SPAN]
COLS_OF_CORE_1 = [[flat(z, 1, y, x) for y in SPAN] for z in SPAN for x in SPAN]
NEAR = ROWS_OF_CORE_0 + COLS_OF_CORE_1
FAR = COLS_OF_CORE_0 + ROWS_OF_CORE_1
STACK = [[flat(z, k, y, x) for z in SPAN] for k in (0, 1) for y in SPAN for x in SPAN]
STACK = [[flat(z, k, y, x) for z in SPAN] for k in (0, 1) for y in SPAN for x in SPAN]
PLANE = [[flat(z, 0, y, x) for y in SPAN for x in SPAN] for z in SPAN] + [
    [flat(z, 1, y, x) for x in SPAN for y in SPAN] for z in SPAN
]


def piece_of(k, y, x):
    return SIDE * y + x if k == 0 else SIDE * x + y


def deals():
    pairs, slices, turned, used = [[], []], [[0] * 128, [0] * 128], [0] * 128, {}
    for z, k, y, x in PLACES:
        here, p = flat(z, k, y, x), piece_of(k, y, x)
        near = x // 2
        turned[here] = near
        for i, block in enumerate((near, 1 - near)):
            plane = (z + y + 2 * k) % SIDE
            core = used.get((i, z, k, block, plane), 0)
            used[i, z, k, block, plane] = core + 1
            there = flat(plane, core, z, 2 * k + block)
            pairs[i].append((there, here))
            slices[i][there] = p
    rows = [[here // 16, here % 16, slices[0][here], slices[1][here], turned[here]] for here in range(128)]
    return pairs, rows


DEALS, PLACE_TABLE = deals()


def partner(z, k, near):
    return z ^ (1 if (k == 0) == near else 3)


def swap_planes(value, near):
    pairs = [(flat(partner(z, k, near), k, y, x), flat(z, k, y, x)) for z, k, y, x in PLACES]
    return lax.ppermute(value, AXES, pairs)


PLANE_ORDER = ((0, 3, 1, 2), (0, 1, 3, 2))


def plane_at(z, core, place):
    return z ^ jnp.where(core == 0, PLANE_ORDER[0][place], PLANE_ORDER[1][place])


def fetch_far(value, d):
    pairs = [(flat(z, k, y + d * (1 - k), x + d * k), flat(z, k, y, x)) for z, k, y, x in PLACES]
    return lax.ppermute(value, AXES, pairs)


def swap_cores(value):
    pairs = [(flat(z, 1 - k, y, x), flat(z, k, y, x)) for z, k, y, x in PLACES]
    return lax.ppermute(value, AXES, pairs)


def exchange(value, groups):
    return lax.all_to_all(value, AXES, 0, 0, axis_index_groups=groups, tiled=True)


def gather(value, groups):
    size = len(groups[0])
    return exchange(jnp.broadcast_to(value[None], (size,) + value.shape), groups)


def scatter_sum(value, groups):
    return jnp.sum(exchange(value, groups), axis=0)


def split(value):
    high = value.astype(jnp.bfloat16)
    return high, (value - high.astype(jnp.float32)).astype(jnp.bfloat16)


def dot3(left, right, dims=(((1,), (0,)), ((), ()))):
    left_high, left_low = split(left)
    right_high, right_low = split(right)

    def dot(a, b):
        return lax.dot_general(a, b, dims, preferred_element_type=jnp.float32)

    return dot(left_high, right_high) + (dot(left_high, right_low) + dot(left_low, right_high))


def split_transposed_kernel(a_ref, out_ref):
    @pl.loop(0, SIDE)
    def _(o):
        parts = [a_ref[pl.ds(pl.multiple_of(BLK * i + GROUP * o, GROUP), GROUP), :] for i in range(2)]
        high, low = split(jnp.concatenate(parts, axis=0))
        out_ref[o, 0] = high.T
        out_ref[o, 1] = low.T


def split_transposed(a):
    rows, cols = a.shape
    out = pl.BlockSpec((SIDE, 2, cols, 2 * GROUP), lambda i: (0, 0, 0, i))
    return pl.pallas_call(
        split_transposed_kernel,
        grid=(rows // (2 * BLK),),
        in_specs=[pl.BlockSpec((2 * BLK, cols), lambda i: (i, 0))],
        out_specs=out,
        out_shape=jax.ShapeDtypeStruct((SIDE, 2, cols, rows // SIDE), jnp.bfloat16),
        compiler_params=pltpu.CompilerParams(vmem_limit_bytes=50 * MIB),
        cost_estimate=pl.CostEstimate(flops=rows * cols, bytes_accessed=8 * rows * cols, transcendentals=0),
    )(a)


def smem(*shape):
    return pl.BlockSpec(memory_space=pltpu.SMEM)


def plan_kernel(place_ref, structure_ref, widths_ref, plan_ref, counts):
    r, c = place_ref[0], place_ref[1]
    chunks = [(widths_ref[i] + LANES - 1) // LANES for i in range(2)]

    def zero(i, _):
        plan_ref[i] = 0
        return 0

    lax.fori_loop(0, PLAN_SIZE, zero, 0)

    def count(col, _):
        total = jnp.int32(0)
        for b in range(4):
            for i in range(2):
                total += jnp.where(structure_ref[i, 4 * col + b] > 0, chunks[i], 0)
        counts[col] = total
        return 0

    lax.fori_loop(0, 16, count, 0)
    most_row = lax.fori_loop(0, 8, lambda i, m: jnp.maximum(m, counts[2 * i] + counts[2 * i + 1]), jnp.int32(0))
    bucket = jnp.int32(0)
    for slots in CAPACITIES[:-1]:
        bucket += jnp.where(most_row > slots, 1, 0)
    plan_ref[BUCKET] = bucket

    def mark(start, base, blocks):
        def one(b, run):
            for q in range(CHUNKS):
                active = (structure_ref[q // SIDE, start + b] > 0) & (q % SIDE < chunks[q // SIDE])
                plan_ref[base + b * CHUNKS + q] = jnp.where(active, run, -1)
                run += jnp.where(active, 1, 0)
            return run

        return lax.fori_loop(0, blocks, one, jnp.int32(0))

    mark(4 * c, OWN, 4)
    mark(8 * r, ROW, 8)
    plan_ref[TURNED] = place_ref[4]
    plan_ref[PLANE_Z] = r // 2
    core = lax.rem(r, 2)
    plan_ref[CORE] = core
    plan_ref[OUTER] = jnp.where(core == 0, c // SIDE, lax.rem(c, SIDE))
    for i in range(2):
        plan_ref[WIDTHS + i] = widths_ref[i]
    for q in range(CHUNKS):
        owner = (q % SIDE) // 2
        apart = (r // 2) ^ (2 * (q // SIDE) + q % 2)
        dest = jnp.int32(0)
        for n in range(1, SIDE):
            dest = jnp.where(apart == PLANE_ORDER[owner][n], n, dest)
        plan_ref[DEST + q] = dest + jnp.where(core == owner, 0, SIDE)


def make_plan(place, structure, widths):
    return pl.pallas_call(
        plan_kernel,
        in_specs=[smem()] * 3,
        out_specs=smem(),
        out_shape=jax.ShapeDtypeStruct((PLAN_SIZE,), jnp.int32),
        scratch_shapes=[pltpu.SMEM((16,), jnp.int32)],
    )(place, structure, widths)


def pack_kernel(place_ref, parent_a, parent_b, child_a, child_b, out_a, out_b):
    out_a[0], out_b[0] = parent_a[...], parent_b[...]
    out_a[1], out_b[1] = child_a[...], child_b[...]


def pack(place, parent, child):
    width = parent.shape[1]
    shaped = [panel.reshape(4, BLK, width) for panel in (parent, child)]
    specs = [pl.BlockSpec((4, SLICE, width), lambda i, place, at=at: (0, place[at], 0)) for at in (2, 3)]
    out = pl.BlockSpec((2, 4, SLICE, width), lambda i, place: (0, 0, 0, 0))
    return pl.pallas_call(
        pack_kernel,
        grid_spec=pltpu.PrefetchScalarGridSpec(
            num_scalar_prefetch=1, grid=(1,), in_specs=specs + specs, out_specs=[out, out]
        ),
        out_shape=[jax.ShapeDtypeStruct((2, 4, SLICE, width), jnp.float32)] * 2,
        compiler_params=pltpu.CompilerParams(vmem_limit_bytes=60 * MIB),
        cost_estimate=pl.CostEstimate(flops=0, bytes_accessed=MIB, transcendentals=0),
    )(place, shaped[0], shaped[0], shaped[1], shaped[1])


def merge_kernel(plan_ref, from_a, from_b, out_ref):
    turned = plan_ref[TURNED] > 0

    @pl.loop(0, 4)
    def _(b):
        for q in range(CHUNKS):
            cols = pl.ds(LANES * (q % SIDE), LANES)
            value_a, value_b = from_a[q // SIDE, b, :, cols], from_b[q // SIDE, b, :, cols]
            for half in range(2):
                slot = plan_ref[ROW + (4 * half + b) * CHUNKS + q]
                value = jnp.where(turned == (half == 0), value_b, value_a)

                @pl.when(slot >= 0)
                def _():
                    for i in SPAN:
                        out_ref[i, slot] = value


def merge(plan, from_a, from_b, slots):
    ins = pl.BlockSpec(from_a.shape, lambda i, plan: (0, 0, 0, 0))
    return pl.pallas_call(
        merge_kernel,
        grid_spec=pltpu.PrefetchScalarGridSpec(
            num_scalar_prefetch=1,
            grid=(1,),
            in_specs=[ins, ins],
            out_specs=pl.BlockSpec((SIDE, slots, SLICE, LANES), lambda i, plan: (0, 0, 0, 0)),
        ),
        out_shape=jax.ShapeDtypeStruct((SIDE, slots, SLICE, LANES), jnp.float32),
        compiler_params=pltpu.CompilerParams(vmem_limit_bytes=16 * MIB),
        cost_estimate=pl.CostEstimate(flops=0, bytes_accessed=4 * MIB, transcendentals=0),
    )(plan, from_a, from_b)


def product_kernel(sizes, has_earlier, plan_ref, *refs):
    count = len(sizes)
    tiles, refs = refs[:count], refs[count:]
    pieces, refs = refs[: sum(sizes)], refs[sum(sizes) :]
    out_refs, (panel_high, panel_low) = refs[has_earlier:-2], refs[-2:]
    tile, depth = tiles[0].shape[2:]

    @pl.when(pl.program_id(0) == 0)
    def _():
        @pl.loop(0, depth // GROUP)
        def _(b):
            for q in range(CHUNKS):
                slot = plan_ref[ROW + b * CHUNKS + q]
                lane = lax.broadcasted_iota(jnp.int32, (GROUP, LANES), 1) + LANES * (q % SIDE)
                kept, slot = (lane < plan_ref[WIDTHS + q // SIDE]) & (slot >= 0), jnp.maximum(slot, 0)
                cols = pl.ds(pl.multiple_of(LANES * plan_ref[DEST + q], LANES), LANES)
                first = 0
                for g, size in enumerate(sizes):
                    values = [ref[:, slot].reshape(-1, LANES) for ref in pieces[first : first + size]]
                    first += size
                    value = values[0] if size == 1 else jnp.concatenate(values, axis=0)
                    high, low = split(jnp.where(kept, value, 0.0))
                    rows = pl.ds(pl.multiple_of(GROUP * b + depth * g, GROUP), GROUP)
                    panel_high[rows, cols] = high
                    panel_low[rows, cols] = low

    width = SIDE * LANES

    def half(i):
        cols = pl.ds(width * i, width) if isinstance(i, int) else pl.ds(pl.multiple_of(width * i, width), width)
        total = None
        for g in range(count):
            rows = pl.ds(depth * g, depth)
            both = tiles[g][0].reshape(2 * tile, depth)
            part = jnp.dot(both, panel_high[rows, cols], preferred_element_type=jnp.float32)
            part = part[:tile] + part[tile:]
            part += jnp.dot(tiles[g][0, 0], panel_low[rows, cols], preferred_element_type=jnp.float32)
            total = part if total is None else total + part
        return [total[:, LANES * q : LANES * (q + 1)] for q in SPAN]

    if len(out_refs) == 1:

        @pl.loop(0, 2)
        def _(i):
            for q, value in enumerate(half(i)):
                out_refs[0][SIDE * i + q] = value + refs[0][SIDE * i + q] if has_earlier else value
    else:
        for i in range(2):
            for q, value in enumerate(half(i)):
                out_refs[2 * i + q // 2][q % 2] = value + refs[0][SIDE * i + q]


def product(plan, split_tile, shifts, groups, earlier=None, is_last=False):
    _, _, cols, depth = split_tile.shape
    tile = 256
    pieces = [piece for group in groups for piece in group]
    whole = pl.BlockSpec((CHUNKS, tile, LANES), lambda i, plan: (0, i, 0))
    pair = pl.BlockSpec((2, tile, LANES), lambda i, plan: (0, i, 0))
    tiles = [
        pl.BlockSpec(
            (1, 2, tile, depth), lambda i, plan, shift=shift: (lax.rem(plan[OUTER] + shift, SIDE), 0, i, 0))
        for shift in shifts
    ]
    kernel = functools.partial(product_kernel, [len(group) for group in groups], earlier is not None)
    return pl.pallas_call(
        kernel,
        grid_spec=pltpu.PrefetchScalarGridSpec(
            num_scalar_prefetch=1,
            grid=(cols // tile,),
            in_specs=tiles
            + [pl.BlockSpec(piece.shape, lambda i, plan: (0, 0, 0, 0)) for piece in pieces]
            + [whole] * (earlier is not None),
            out_specs=[pair] * 4 if is_last else whole,
            scratch_shapes=[pltpu.VMEM((depth * len(shifts), CHUNKS * LANES), jnp.bfloat16)] * 2,
        ),
        out_shape=[jax.ShapeDtypeStruct((2, cols, LANES), jnp.float32)] * 4
        if is_last
        else jax.ShapeDtypeStruct((CHUNKS, cols, LANES), jnp.float32),
        compiler_params=pltpu.CompilerParams(vmem_limit_bytes=32 * MIB),
        cost_estimate=pl.CostEstimate(
            flops=6 * len(shifts) * depth * cols * CHUNKS * LANES, bytes_accessed=12 * MIB, transcendentals=0
        ),
    )(plan, *[split_tile] * len(shifts), *pieces, *([] if earlier is None else [earlier]))


def products(slots):
    def run(plan, split_tile, dealt):
        near = exchange(merge(plan, *dealt, slots), NEAR)
        ahead, behind = fetch_far(near, 1), fetch_far(near, 3)
        total = product(plan, split_tile, (0,), ((near,),))
        total, ahead, behind = lax.optimization_barrier((total, ahead, behind))
        far_first, far_last = fetch_far(ahead[:2], 1), fetch_far(behind[2:], 3)
        total = product(plan, split_tile, (1, 3), ((ahead,), (behind,)), total)
        return product(plan, split_tile, (2,), ((far_first, far_last),), total, True)

    return run


def turn_kernel(plan_ref, parent_ref, child_ref, high_ref, low_ref):
    first = slab_chunk(plan_ref[PLANE_Z], plan_ref[CORE])
    t = pl.program_id(0)
    q = lax.rem(first + t, CHUNKS)
    lane = lax.broadcasted_iota(jnp.int32, (BLK, LANES), 1)
    for panel, ref in enumerate((parent_ref, child_ref)):

        @pl.when(q // SIDE == panel)
        def _():
            start = LANES * lax.rem(q, SIDE)
            cols = pl.ds(pl.multiple_of(start, LANES), LANES)
            mask = jnp.where(lane + start < plan_ref[WIDTHS + panel], 1.0, 0.0)
            for b in range(4):
                keep = jnp.where(plan_ref[OWN + b * CHUNKS + SIDE * panel] >= 0, 1.0, 0.0)
                rows = pl.ds(BLK * b, BLK)
                high, low = split(ref[rows, cols] * mask * keep)
                high_ref[:, rows] = high.T
                low_ref[:, rows] = low.T


def turn(plan, parent, child):
    rows, width = parent.shape
    out = pl.BlockSpec((LANES, rows), lambda t, plan: (t, 0))
    panel = pl.BlockSpec((rows, width), lambda t, plan: (0, 0))
    return pl.pallas_call(
        turn_kernel,
        grid_spec=pltpu.PrefetchScalarGridSpec(
            num_scalar_prefetch=1, grid=(5,), in_specs=[panel, panel], out_specs=[out, out]
        ),
        out_shape=[jax.ShapeDtypeStruct((5 * LANES, rows), jnp.bfloat16)] * 2,
        compiler_params=pltpu.CompilerParams(vmem_limit_bytes=48 * MIB),
        cost_estimate=pl.CostEstimate(flops=MIB, bytes_accessed=8 * MIB, transcendentals=0),
    )(plan, parent, child)


def slab_kernel(kept_ref, passed_ref, high_ref, low_ref, slab_ref, sums_ref):
    slab = kept_ref[...] + passed_ref[...]
    slab_ref[...] = slab
    slab_high, slab_low = split(slab)
    total = jnp.dot(high_ref[...], slab_high, preferred_element_type=jnp.float32)
    total += jnp.dot(high_ref[...], slab_low, preferred_element_type=jnp.float32)
    sums_ref[...] = total + jnp.dot(low_ref[...], slab_high, preferred_element_type=jnp.float32)


def finish_slab(kept, passed, high, low):
    rows, width = kept.shape
    return pl.pallas_call(
        slab_kernel,
        out_shape=[
            jax.ShapeDtypeStruct((rows, width), jnp.float32),
            jax.ShapeDtypeStruct((high.shape[0], width), jnp.float32),
        ],
        compiler_params=pltpu.CompilerParams(vmem_limit_bytes=16 * MIB),
        cost_estimate=pl.CostEstimate(flops=6 * high.size * width, bytes_accessed=6 * MIB, transcendentals=0),
    )(kept, passed, high, low)


def slab_chunk(z, k):
    return SIDE * (z // 2) + 2 * k + lax.rem(z, 2)


def masked_cross(plan_ref, cross_ref):
    rows = lax.broadcasted_iota(jnp.int32, cross_ref.shape, 0)
    cols = lax.broadcasted_iota(jnp.int32, cross_ref.shape, 1)
    keep = jnp.where(rows < plan_ref[WIDTHS], 1.0, 0.0) * jnp.where(cols < plan_ref[WIDTHS + 1], 1.0, 0.0)
    return cross_ref[...] * keep


def masked_square(ref, width):
    rows = lax.broadcasted_iota(jnp.int32, ref.shape, 0)
    cols = lax.broadcasted_iota(jnp.int32, ref.shape, 1)
    return ref[...] * (jnp.where(rows < width, 1.0, 0.0) * jnp.where(cols < width, 1.0, 0.0))


def rows_kernel(plan_ref, own_a, own_b, other_a, other_b, cross_ref, inv_sp_ref, inv_sc_ref, total):
    z, k = plan_ref[PLANE_Z], plan_ref[CORE]
    for refs, core in (((own_a, own_b), k), ((other_a, other_b), 1 - k)):
        for i in SPAN:
            start = LANES * slab_chunk(plane_at(z, core, i), core)
            total[:, pl.ds(pl.multiple_of(start, LANES), LANES)] = refs[i // 2][i % 2]
    width = cross_ref.shape[0]
    block = OWN + pl.program_id(0) * CHUNKS
    keep = [jnp.where(plan_ref[block + SIDE * i] >= 0, 1.0, 0.0) for i in range(2)]
    inv_sp = -total[:, :width] * keep[0]
    inv_sp_ref[...] = inv_sp
    inv_sc_ref[...] = -(total[:, width:] + dot3(inv_sp, masked_cross(plan_ref, cross_ref))) * keep[1]


def finish_rows(plan, slabs, cross):
    _, rows, _ = slabs[0].shape
    width = cross.shape[0]
    pair = pl.BlockSpec((2, BLK, LANES), lambda i, plan: (0, i, 0))
    whole = pl.BlockSpec((BLK, width), lambda i, plan: (i, 0))
    return pl.pallas_call(
        rows_kernel,
        grid_spec=pltpu.PrefetchScalarGridSpec(
            num_scalar_prefetch=1,
            grid=(rows // BLK,),
            in_specs=[pair] * 4 + [pl.BlockSpec((width, width), lambda i, plan: (0, 0))],
            out_specs=[whole, whole],
            scratch_shapes=[pltpu.VMEM((BLK, 2 * width), jnp.float32)],
        ),
        out_shape=[jax.ShapeDtypeStruct((rows, width), jnp.float32)] * 2,
        compiler_params=pltpu.CompilerParams(vmem_limit_bytes=32 * MIB),
        cost_estimate=pl.CostEstimate(flops=6 * rows * width * width, bytes_accessed=16 * rows * width, transcendentals=0),
    )(plan, *slabs, cross)


def blocks_kernel(
    plan_ref, own_ref, other_ref, cross_ref, parent_ref, child_ref, inv_pp_ref, inv_pc_ref, inv_cc_ref, slab, total
):
    share = own_ref.shape[2]
    k = plan_ref[CORE]
    for ref, core in ((own_ref, k), (other_ref, 1 - k)):
        for z in SPAN:
            j = SIDE * (z // 2) + 2 * core + z % 2
            for i in SPAN:
                slab[j, pl.ds(share * i, share), :] = ref[i, z]
    for j in range(CHUNKS):
        for i in range(CHUNKS):
            t = (i - j) % CHUNKS
            if t <= 4:
                block = slab[j, pl.ds(LANES * t, LANES), :]
            else:
                block = slab[i, pl.ds(LANES * (CHUNKS - t), LANES), :].T
            total[pl.ds(LANES * i, LANES), pl.ds(LANES * j, LANES)] = block
    width = cross_ref.shape[0]
    cross = masked_cross(plan_ref, cross_ref)
    inv_pp = masked_square(parent_ref, plan_ref[WIDTHS]) + total[:width, :width]
    inv_pp_ref[...] = inv_pp
    inv_pc = total[:width, width:] - dot3(inv_pp, cross)
    inv_pc_ref[...] = inv_pc
    last = dot3(cross, inv_pc, (((0,), (0,)), ((), ()))) + dot3(total[width:, :width], cross)
    inv_cc_ref[...] = masked_square(child_ref, plan_ref[WIDTHS + 1]) + total[width:, width:] - last


def finish_blocks(plan, own, other, cross, parent, child):
    width = cross.shape[0]
    square = pl.BlockSpec((width, width), lambda i, plan: (0, 0))
    sums = pl.BlockSpec(own.shape, lambda i, plan: (0, 0, 0, 0))
    return pl.pallas_call(
        blocks_kernel,
        grid_spec=pltpu.PrefetchScalarGridSpec(
            num_scalar_prefetch=1,
            grid=(1,),
            in_specs=[sums, sums] + [square] * 3,
            out_specs=[square] * 3,
            scratch_shapes=[
                pltpu.VMEM((CHUNKS, 5 * LANES, LANES), jnp.float32),
                pltpu.VMEM((2 * width, 2 * width), jnp.float32),
            ],
        ),
        out_shape=[jax.ShapeDtypeStruct((width, width), jnp.float32)] * 3,
        compiler_params=pltpu.CompilerParams(vmem_limit_bytes=32 * MIB),
        cost_estimate=pl.CostEstimate(flops=18 * width**3, bytes_accessed=40 * width * width, transcendentals=0),
    )(plan, own, other, cross, parent, child)


def per_device(
    ancestor_inv, lhat_parent, lhat_child, lhat_cross, diag_parent, diag_child, structure, widths
):
    here = lax.axis_index("prow") * 16 + lax.axis_index("pcol")
    place = lax.dynamic_index_in_dim(jnp.array(PLACE_TABLE, jnp.int32), here, 0, keepdims=False)
    sent = pack(place, lhat_parent, lhat_child)
    dealt = [lax.ppermute(value, AXES, pairs) for value, pairs in zip(sent, DEALS)]
    plan, split_tile, *dealt = lax.optimization_barrier(
        (make_plan(place, structure, widths), split_transposed(ancestor_inv), *dealt))
    kept, passed, send_kept, send_passed = lax.switch(
        plan[BUCKET], [products(slots) for slots in CAPACITIES], plan, split_tile, dealt)

    passed = swap_planes(passed + swap_cores(send_passed), True)
    kept = kept + swap_cores(send_kept)
    kept, passed, high, low = lax.optimization_barrier((kept, passed, *turn(plan, lhat_parent, lhat_child)))
    kept = kept + passed
    slab, sums = finish_slab(kept[0], swap_planes(kept[1], False), high, low)

    far_slab = swap_planes(slab, False)
    sums = scatter_sum(sums.reshape(SIDE, -1, LANES), NEAR)
    far_slab, sums = lax.optimization_barrier((far_slab, sums))
    first = jnp.stack([slab, far_slab])
    second, other_first = swap_planes(first, True), swap_cores(first)
    sums = jnp.sum(gather(sums, FAR), axis=0)
    sums = gather(sums, STACK)
    second, other_first, sums = lax.optimization_barrier((second, other_first, sums))
    other_second = swap_cores(second)
    sums = gather(sums, NEAR)
    other_second, sums = lax.optimization_barrier((other_second, sums))
    other_sums = swap_cores(sums)
    inv_sp, inv_sc = finish_rows(plan, (first, second, other_first, other_second), lhat_cross)
    inv_sp, inv_sc, other_sums = lax.optimization_barrier((inv_sp, inv_sc, other_sums))
    inv_pp, inv_pc, inv_cc = finish_blocks(plan, sums, other_sums, lhat_cross, diag_parent, diag_child)
    return (inv_sp, inv_pp, inv_sc, inv_pc, inv_cc)


def solution(mesh):
    return jax.shard_map(
        per_device,
        mesh=mesh,
        in_specs=(P("prow", "pcol"), P("pcol", None), P("pcol", None), P(), P(), P(), P(), P()),
        out_specs=(P("pcol", None), P(), P("pcol", None), P(), P()),
        check_vma=False,
    )
```

```python
import functools

import jax
import jax.numpy as jnp
from jax import lax
from jax.experimental import pallas as pl
from jax.experimental.pallas import tpu as pltpu
from jax.sharding import PartitionSpec as P

BLK = 256
AXES = ("prow", "pcol")
SIDE = 4
LANES = 128
MIB = 1 << 20
SPAN = range(SIDE)
CHUNKS = 2 * SIDE
SLICE = 16
GROUP = SIDE * SLICE
CAPACITIES = (36, 46, 64)
BUCKET, TURNED, PLANE_Z, CORE, OUTER = range(5)
OWN, ROW, WIDTHS, DEST, PLAN_SIZE = 16, 48, 112, 114, 128


def flat(z, k, y, x):
    return ((z % SIDE) * 2 + k) * SIDE * SIDE + (y % SIDE) * SIDE + x % SIDE


PLACES = [(z, k, y, x) for z in SPAN for k in (0, 1) for y in SPAN for x in SPAN]
ROWS_OF_CORE_0 = [[flat(z, 0, y, x) for x in SPAN] for z in SPAN for y in SPAN]
COLS_OF_CORE_0 = [[flat(z, 0, y, x) for y in SPAN] for z in SPAN for x in SPAN]
ROWS_OF_CORE_1 = [[flat(z, 1, y, x) for x in SPAN] for z in SPAN for y in SPAN]
COLS_OF_CORE_1 = [[flat(z, 1, y, x) for y in SPAN] for z in SPAN for x in SPAN]
NEAR = ROWS_OF_CORE_0 + COLS_OF_CORE_1
FAR = COLS_OF_CORE_0 + ROWS_OF_CORE_1
STACK = [[flat(z, k, y, x) for z in SPAN] for k in (0, 1) for y in SPAN for x in SPAN]
STACK = [[flat(z, k, y, x) for z in SPAN] for k in (0, 1) for y in SPAN for x in SPAN]
PLANE = [[flat(z, 0, y, x) for y in SPAN for x in SPAN] for z in SPAN] + [
    [flat(z, 1, y, x) for x in SPAN for y in SPAN] for z in SPAN
]


def piece_of(k, y, x):
    return SIDE * y + x if k == 0 else SIDE * x + y


def deals():
    pairs, slices, turned, used = [[], []], [[0] * 128, [0] * 128], [0] * 128, {}
    for z, k, y, x in PLACES:
        here, p = flat(z, k, y, x), piece_of(k, y, x)
        near = x // 2
        turned[here] = near
        for i, block in enumerate((near, 1 - near)):
            plane = (z + y + 2 * k) % SIDE
            core = used.get((i, z, k, block, plane), 0)
            used[i, z, k, block, plane] = core + 1
            there = flat(plane, core, z, 2 * k + block)
            pairs[i].append((there, here))
            slices[i][there] = p
    rows = [[here // 16, here % 16, slices[0][here], slices[1][here], turned[here]] for here in range(128)]
    return pairs, rows


DEALS, PLACE_TABLE = deals()


def partner(z, k, near):
    return z ^ (1 if (k == 0) == near else 3)


def swap_planes(value, near):
    pairs = [(flat(partner(z, k, near), k, y, x), flat(z, k, y, x)) for z, k, y, x in PLACES]
    return lax.ppermute(value, AXES, pairs)


PLANE_ORDER = ((0, 3, 1, 2), (0, 1, 3, 2))


def plane_at(z, core, place):
    return z ^ jnp.where(core == 0, PLANE_ORDER[0][place], PLANE_ORDER[1][place])


def fetch_far(value, d):
    pairs = [(flat(z, k, y + d * (1 - k), x + d * k), flat(z, k, y, x)) for z, k, y, x in PLACES]
    return lax.ppermute(value, AXES, pairs)


def swap_cores(value):
    pairs = [(flat(z, 1 - k, y, x), flat(z, k, y, x)) for z, k, y, x in PLACES]
    return lax.ppermute(value, AXES, pairs)


def exchange(value, groups):
    return lax.all_to_all(value, AXES, 0, 0, axis_index_groups=groups, tiled=True)


def gather(value, groups):
    size = len(groups[0])
    return exchange(jnp.broadcast_to(value[None], (size,) + value.shape), groups)


def scatter_sum(value, groups):
    return jnp.sum(exchange(value, groups), axis=0)


def split(value):
    high = value.astype(jnp.bfloat16)
    return high, (value - high.astype(jnp.float32)).astype(jnp.bfloat16)


def dot3(left, right, dims=(((1,), (0,)), ((), ()))):
    left_high, left_low = split(left)
    right_high, right_low = split(right)

    def dot(a, b):
        return lax.dot_general(a, b, dims, preferred_element_type=jnp.float32)

    return dot(left_high, right_high) + (dot(left_high, right_low) + dot(left_low, right_high))


def split_transposed_kernel(a_ref, out_ref):
    @pl.loop(0, SIDE)
    def _(o):
        parts = [a_ref[pl.ds(pl.multiple_of(BLK * i + GROUP * o, GROUP), GROUP), :] for i in range(2)]
        high, low = split(jnp.concatenate(parts, axis=0))
        out_ref[0, o, 0] = high.T
        out_ref[0, o, 1] = low.T


def split_transposed(a):
    rows, cols = a.shape
    steps = rows // (2 * BLK)
    out = pl.BlockSpec((1, SIDE, 2, cols, 2 * GROUP), lambda i: (i, 0, 0, 0, 0))
    return pl.pallas_call(
        split_transposed_kernel,
        grid=(steps,),
        in_specs=[pl.BlockSpec((2 * BLK, cols), lambda i: (i, 0))],
        out_specs=out,
        out_shape=jax.ShapeDtypeStruct((steps, SIDE, 2, cols, 2 * GROUP), jnp.bfloat16),
        compiler_params=pltpu.CompilerParams(vmem_limit_bytes=50 * MIB),
        cost_estimate=pl.CostEstimate(flops=rows * cols, bytes_accessed=8 * rows * cols, transcendentals=0),
    )(a)


def smem(*shape):
    return pl.BlockSpec(memory_space=pltpu.SMEM)


def plan_kernel(place_ref, structure_ref, widths_ref, plan_ref, counts):
    r, c = place_ref[0], place_ref[1]
    chunks = [(widths_ref[i] + LANES - 1) // LANES for i in range(2)]

    def zero(i, _):
        plan_ref[i] = 0
        return 0

    lax.fori_loop(0, PLAN_SIZE, zero, 0)

    def count(col, _):
        total = jnp.int32(0)
        for b in range(4):
            for i in range(2):
                total += jnp.where(structure_ref[i, 4 * col + b] > 0, chunks[i], 0)
        counts[col] = total
        return 0

    lax.fori_loop(0, 16, count, 0)
    most_row = lax.fori_loop(0, 8, lambda i, m: jnp.maximum(m, counts[2 * i] + counts[2 * i + 1]), jnp.int32(0))
    bucket = jnp.int32(0)
    for slots in CAPACITIES[:-1]:
        bucket += jnp.where(most_row > slots, 1, 0)
    plan_ref[BUCKET] = bucket

    def mark(start, base, blocks):
        def one(b, run):
            for q in range(CHUNKS):
                active = (structure_ref[q // SIDE, start + b] > 0) & (q % SIDE < chunks[q // SIDE])
                plan_ref[base + b * CHUNKS + q] = jnp.where(active, run, -1)
                run += jnp.where(active, 1, 0)
            return run

        return lax.fori_loop(0, blocks, one, jnp.int32(0))

    mark(4 * c, OWN, 4)
    mark(8 * r, ROW, 8)
    plan_ref[TURNED] = place_ref[4]
    plan_ref[PLANE_Z] = r // 2
    core = lax.rem(r, 2)
    plan_ref[CORE] = core
    plan_ref[OUTER] = jnp.where(core == 0, c // SIDE, lax.rem(c, SIDE))
    for i in range(2):
        plan_ref[WIDTHS + i] = widths_ref[i]
    for q in range(CHUNKS):
        owner = (q % SIDE) // 2
        apart = (r // 2) ^ (2 * (q // SIDE) + q % 2)
        dest = jnp.int32(0)
        for n in range(1, SIDE):
            dest = jnp.where(apart == PLANE_ORDER[owner][n], n, dest)
        plan_ref[DEST + q] = dest + jnp.where(core == owner, 0, SIDE)


def make_plan(place, structure, widths):
    return pl.pallas_call(
        plan_kernel,
        in_specs=[smem()] * 3,
        out_specs=smem(),
        out_shape=jax.ShapeDtypeStruct((PLAN_SIZE,), jnp.int32),
        scratch_shapes=[pltpu.SMEM((16,), jnp.int32)],
    )(place, structure, widths)


def pack_kernel(place_ref, parent_a, parent_b, child_a, child_b, out_a, out_b):
    out_a[0], out_b[0] = parent_a[...], parent_b[...]
    out_a[1], out_b[1] = child_a[...], child_b[...]


def pack(place, parent, child):
    width = parent.shape[1]
    shaped = [panel.reshape(4, BLK, width) for panel in (parent, child)]
    specs = [pl.BlockSpec((4, SLICE, width), lambda i, place, at=at: (0, place[at], 0)) for at in (2, 3)]
    out = pl.BlockSpec((2, 4, SLICE, width), lambda i, place: (0, 0, 0, 0))
    return pl.pallas_call(
        pack_kernel,
        grid_spec=pltpu.PrefetchScalarGridSpec(
            num_scalar_prefetch=1, grid=(1,), in_specs=specs + specs, out_specs=[out, out]
        ),
        out_shape=[jax.ShapeDtypeStruct((2, 4, SLICE, width), jnp.float32)] * 2,
        compiler_params=pltpu.CompilerParams(vmem_limit_bytes=60 * MIB),
        cost_estimate=pl.CostEstimate(flops=0, bytes_accessed=MIB, transcendentals=0),
    )(place, shaped[0], shaped[0], shaped[1], shaped[1])


def merge_kernel(plan_ref, from_a, from_b, out_ref):
    turned = plan_ref[TURNED] > 0

    @pl.loop(0, 4)
    def _(b):
        for q in range(CHUNKS):
            cols = pl.ds(LANES * (q % SIDE), LANES)
            value_a, value_b = from_a[q // SIDE, b, :, cols], from_b[q // SIDE, b, :, cols]
            for half in range(2):
                slot = plan_ref[ROW + (4 * half + b) * CHUNKS + q]
                value = jnp.where(turned == (half == 0), value_b, value_a)

                @pl.when(slot >= 0)
                def _():
                    for i in SPAN:
                        out_ref[i, slot] = value


def merge(plan, from_a, from_b, slots):
    ins = pl.BlockSpec(from_a.shape, lambda i, plan: (0, 0, 0, 0))
    return pl.pallas_call(
        merge_kernel,
        grid_spec=pltpu.PrefetchScalarGridSpec(
            num_scalar_prefetch=1,
            grid=(1,),
            in_specs=[ins, ins],
            out_specs=pl.BlockSpec((SIDE, slots, SLICE, LANES), lambda i, plan: (0, 0, 0, 0)),
        ),
        out_shape=jax.ShapeDtypeStruct((SIDE, slots, SLICE, LANES), jnp.float32),
        compiler_params=pltpu.CompilerParams(vmem_limit_bytes=16 * MIB),
        cost_estimate=pl.CostEstimate(flops=0, bytes_accessed=4 * MIB, transcendentals=0),
    )(plan, from_a, from_b)


def product_kernel(sizes, has_earlier, plan_ref, *refs):
    count = len(sizes)
    tiles, refs = refs[:count], refs[count:]
    pieces, refs = refs[: sum(sizes)], refs[sum(sizes) :]
    out_refs, (panel_high, panel_low) = refs[has_earlier:-2], refs[-2:]
    steps, _, _, tile, lanes = tiles[0].shape
    depth = steps * lanes

    @pl.when(pl.program_id(0) == 0)
    def _():
        @pl.loop(0, depth // GROUP)
        def _(b):
            for q in range(CHUNKS):
                slot = plan_ref[ROW + b * CHUNKS + q]
                lane = lax.broadcasted_iota(jnp.int32, (GROUP, LANES), 1) + LANES * (q % SIDE)
                kept, slot = (lane < plan_ref[WIDTHS + q // SIDE]) & (slot >= 0), jnp.maximum(slot, 0)
                cols = pl.ds(pl.multiple_of(LANES * plan_ref[DEST + q], LANES), LANES)
                first = 0
                for g, size in enumerate(sizes):
                    values = [ref[:, slot].reshape(-1, LANES) for ref in pieces[first : first + size]]
                    first += size
                    value = values[0] if size == 1 else jnp.concatenate(values, axis=0)
                    high, low = split(jnp.where(kept, value, 0.0))
                    rows = pl.ds(pl.multiple_of(GROUP * b + depth * g, GROUP), GROUP)
                    panel_high[rows, cols] = high
                    panel_low[rows, cols] = low

    width = SIDE * LANES

    def half(i):
        cols = pl.ds(width * i, width) if isinstance(i, int) else pl.ds(pl.multiple_of(width * i, width), width)
        total = None
        for g in range(count):
            rows = pl.ds(depth * g, depth)
            both = jnp.concatenate([tiles[g][n, 0].reshape(2 * tile, lanes) for n in range(steps)], axis=1)
            part = jnp.dot(both, panel_high[rows, cols], preferred_element_type=jnp.float32)
            part = part[:tile] + part[tile:]
            part += jnp.dot(both[:tile], panel_low[rows, cols], preferred_element_type=jnp.float32)
            total = part if total is None else total + part
        return [total[:, LANES * q : LANES * (q + 1)] for q in SPAN]

    if len(out_refs) == 1:

        @pl.loop(0, 2)
        def _(i):
            for q, value in enumerate(half(i)):
                out_refs[0][SIDE * i + q] = value + refs[0][SIDE * i + q] if has_earlier else value
    else:
        for i in range(2):
            for q, value in enumerate(half(i)):
                out_refs[2 * i + q // 2][q % 2] = value + refs[0][SIDE * i + q]


def product(plan, split_tile, shifts, groups, earlier=None, is_last=False):
    steps, _, _, cols, lanes = split_tile.shape
    depth = steps * lanes
    tile = 256
    pieces = [piece for group in groups for piece in group]
    whole = pl.BlockSpec((CHUNKS, tile, LANES), lambda i, plan: (0, i, 0))
    pair = pl.BlockSpec((2, tile, LANES), lambda i, plan: (0, i, 0))
    tiles = [
        pl.BlockSpec(
            (steps, 1, 2, tile, lanes), lambda i, plan, shift=shift: (0, lax.rem(plan[OUTER] + shift, SIDE), 0, i, 0))
        for shift in shifts
    ]
    kernel = functools.partial(product_kernel, [len(group) for group in groups], earlier is not None)
    return pl.pallas_call(
        kernel,
        grid_spec=pltpu.PrefetchScalarGridSpec(
            num_scalar_prefetch=1,
            grid=(cols // tile,),
            in_specs=tiles
            + [pl.BlockSpec(piece.shape, lambda i, plan: (0, 0, 0, 0)) for piece in pieces]
            + [whole] * (earlier is not None),
            out_specs=[pair] * 4 if is_last else whole,
            scratch_shapes=[pltpu.VMEM((depth * len(shifts), CHUNKS * LANES), jnp.bfloat16)] * 2,
        ),
        out_shape=[jax.ShapeDtypeStruct((2, cols, LANES), jnp.float32)] * 4
        if is_last
        else jax.ShapeDtypeStruct((CHUNKS, cols, LANES), jnp.float32),
        compiler_params=pltpu.CompilerParams(vmem_limit_bytes=32 * MIB),
        cost_estimate=pl.CostEstimate(
            flops=6 * len(shifts) * depth * cols * CHUNKS * LANES, bytes_accessed=12 * MIB, transcendentals=0
        ),
    )(plan, *[split_tile] * len(shifts), *pieces, *([] if earlier is None else [earlier]))


def products(slots):
    def run(plan, split_tile, dealt):
        near = exchange(merge(plan, *dealt, slots), NEAR)
        ahead, behind = fetch_far(near, 1), fetch_far(near, 3)
        total = product(plan, split_tile, (0,), ((near,),))
        total, ahead, behind = lax.optimization_barrier((total, ahead, behind))
        far_first, far_last = fetch_far(ahead[:2], 1), fetch_far(behind[2:], 3)
        total = product(plan, split_tile, (1, 3), ((ahead,), (behind,)), total)
        return product(plan, split_tile, (2,), ((far_first, far_last),), total, True)

    return run


def turn_kernel(plan_ref, parent_ref, child_ref, high_ref, low_ref):
    first = slab_chunk(plan_ref[PLANE_Z], plan_ref[CORE])
    t = pl.program_id(0)
    q = lax.rem(first + t, CHUNKS)
    lane = lax.broadcasted_iota(jnp.int32, (BLK, LANES), 1)
    for panel, ref in enumerate((parent_ref, child_ref)):

        @pl.when(q // SIDE == panel)
        def _():
            start = LANES * lax.rem(q, SIDE)
            cols = pl.ds(pl.multiple_of(start, LANES), LANES)
            mask = jnp.where(lane + start < plan_ref[WIDTHS + panel], 1.0, 0.0)
            for b in range(4):
                keep = jnp.where(plan_ref[OWN + b * CHUNKS + SIDE * panel] >= 0, 1.0, 0.0)
                rows = pl.ds(BLK * b, BLK)
                high, low = split(ref[rows, cols] * mask * keep)
                high_ref[:, rows] = high.T
                low_ref[:, rows] = low.T


def turn(plan, parent, child):
    rows, width = parent.shape
    out = pl.BlockSpec((LANES, rows), lambda t, plan: (t, 0))
    panel = pl.BlockSpec((rows, width), lambda t, plan: (0, 0))
    return pl.pallas_call(
        turn_kernel,
        grid_spec=pltpu.PrefetchScalarGridSpec(
            num_scalar_prefetch=1, grid=(5,), in_specs=[panel, panel], out_specs=[out, out]
        ),
        out_shape=[jax.ShapeDtypeStruct((5 * LANES, rows), jnp.bfloat16)] * 2,
        compiler_params=pltpu.CompilerParams(vmem_limit_bytes=48 * MIB),
        cost_estimate=pl.CostEstimate(flops=MIB, bytes_accessed=8 * MIB, transcendentals=0),
    )(plan, parent, child)


def slab_kernel(kept_ref, passed_ref, high_ref, low_ref, slab_ref, sums_ref):
    slab = kept_ref[...] + passed_ref[...]
    slab_ref[...] = slab
    slab_high, slab_low = split(slab)
    total = jnp.dot(high_ref[...], slab_high, preferred_element_type=jnp.float32)
    total += jnp.dot(high_ref[...], slab_low, preferred_element_type=jnp.float32)
    sums_ref[...] = total + jnp.dot(low_ref[...], slab_high, preferred_element_type=jnp.float32)


def finish_slab(kept, passed, high, low):
    rows, width = kept.shape
    return pl.pallas_call(
        slab_kernel,
        out_shape=[
            jax.ShapeDtypeStruct((rows, width), jnp.float32),
            jax.ShapeDtypeStruct((high.shape[0], width), jnp.float32),
        ],
        compiler_params=pltpu.CompilerParams(vmem_limit_bytes=16 * MIB),
        cost_estimate=pl.CostEstimate(flops=6 * high.size * width, bytes_accessed=6 * MIB, transcendentals=0),
    )(kept, passed, high, low)


def slab_chunk(z, k):
    return SIDE * (z // 2) + 2 * k + lax.rem(z, 2)


def masked_cross(plan_ref, cross_ref):
    rows = lax.broadcasted_iota(jnp.int32, cross_ref.shape, 0)
    cols = lax.broadcasted_iota(jnp.int32, cross_ref.shape, 1)
    keep = jnp.where(rows < plan_ref[WIDTHS], 1.0, 0.0) * jnp.where(cols < plan_ref[WIDTHS + 1], 1.0, 0.0)
    return cross_ref[...] * keep


def masked_square(ref, width):
    rows = lax.broadcasted_iota(jnp.int32, ref.shape, 0)
    cols = lax.broadcasted_iota(jnp.int32, ref.shape, 1)
    return ref[...] * (jnp.where(rows < width, 1.0, 0.0) * jnp.where(cols < width, 1.0, 0.0))


def rows_kernel(plan_ref, own_a, own_b, other_a, other_b, cross_ref, inv_sp_ref, inv_sc_ref, total):
    z, k = plan_ref[PLANE_Z], plan_ref[CORE]
    for refs, core in (((own_a, own_b), k), ((other_a, other_b), 1 - k)):
        for i in SPAN:
            start = LANES * slab_chunk(plane_at(z, core, i), core)
            total[:, pl.ds(pl.multiple_of(start, LANES), LANES)] = refs[i // 2][i % 2]
    width = cross_ref.shape[0]
    block = OWN + pl.program_id(0) * CHUNKS
    keep = [jnp.where(plan_ref[block + SIDE * i] >= 0, 1.0, 0.0) for i in range(2)]
    inv_sp = -total[:, :width] * keep[0]
    inv_sp_ref[...] = inv_sp
    inv_sc_ref[...] = -(total[:, width:] + dot3(inv_sp, masked_cross(plan_ref, cross_ref))) * keep[1]


def finish_rows(plan, slabs, cross):
    _, rows, _ = slabs[0].shape
    width = cross.shape[0]
    pair = pl.BlockSpec((2, BLK, LANES), lambda i, plan: (0, i, 0))
    whole = pl.BlockSpec((BLK, width), lambda i, plan: (i, 0))
    return pl.pallas_call(
        rows_kernel,
        grid_spec=pltpu.PrefetchScalarGridSpec(
            num_scalar_prefetch=1,
            grid=(rows // BLK,),
            in_specs=[pair] * 4 + [pl.BlockSpec((width, width), lambda i, plan: (0, 0))],
            out_specs=[whole, whole],
            scratch_shapes=[pltpu.VMEM((BLK, 2 * width), jnp.float32)],
        ),
        out_shape=[jax.ShapeDtypeStruct((rows, width), jnp.float32)] * 2,
        compiler_params=pltpu.CompilerParams(vmem_limit_bytes=32 * MIB),
        cost_estimate=pl.CostEstimate(flops=6 * rows * width * width, bytes_accessed=16 * rows * width, transcendentals=0),
    )(plan, *slabs, cross)


def blocks_kernel(
    plan_ref, own_ref, other_ref, cross_ref, parent_ref, child_ref, inv_pp_ref, inv_pc_ref, inv_cc_ref, slab, total
):
    share = own_ref.shape[2]
    k = plan_ref[CORE]
    for ref, core in ((own_ref, k), (other_ref, 1 - k)):
        for z in SPAN:
            j = SIDE * (z // 2) + 2 * core + z % 2
            for i in SPAN:
                slab[j, pl.ds(share * i, share), :] = ref[i, z]
    for j in range(CHUNKS):
        for i in range(CHUNKS):
            t = (i - j) % CHUNKS
            if t <= 4:
                block = slab[j, pl.ds(LANES * t, LANES), :]
            else:
                block = slab[i, pl.ds(LANES * (CHUNKS - t), LANES), :].T
            total[pl.ds(LANES * i, LANES), pl.ds(LANES * j, LANES)] = block
    width = cross_ref.shape[0]
    cross = masked_cross(plan_ref, cross_ref)
    inv_pp = masked_square(parent_ref, plan_ref[WIDTHS]) + total[:width, :width]
    inv_pp_ref[...] = inv_pp
    inv_pc = total[:width, width:] - dot3(inv_pp, cross)
    inv_pc_ref[...] = inv_pc
    last = dot3(cross, inv_pc, (((0,), (0,)), ((), ()))) + dot3(total[width:, :width], cross)
    inv_cc_ref[...] = masked_square(child_ref, plan_ref[WIDTHS + 1]) + total[width:, width:] - last


def finish_blocks(plan, own, other, cross, parent, child):
    width = cross.shape[0]
    square = pl.BlockSpec((width, width), lambda i, plan: (0, 0))
    sums = pl.BlockSpec(own.shape, lambda i, plan: (0, 0, 0, 0))
    return pl.pallas_call(
        blocks_kernel,
        grid_spec=pltpu.PrefetchScalarGridSpec(
            num_scalar_prefetch=1,
            grid=(1,),
            in_specs=[sums, sums] + [square] * 3,
            out_specs=[square] * 3,
            scratch_shapes=[
                pltpu.VMEM((CHUNKS, 5 * LANES, LANES), jnp.float32),
                pltpu.VMEM((2 * width, 2 * width), jnp.float32),
            ],
        ),
        out_shape=[jax.ShapeDtypeStruct((width, width), jnp.float32)] * 3,
        compiler_params=pltpu.CompilerParams(vmem_limit_bytes=32 * MIB),
        cost_estimate=pl.CostEstimate(flops=18 * width**3, bytes_accessed=40 * width * width, transcendentals=0),
    )(plan, own, other, cross, parent, child)


def per_device(
    ancestor_inv, lhat_parent, lhat_child, lhat_cross, diag_parent, diag_child, structure, widths
):
    here = lax.axis_index("prow") * 16 + lax.axis_index("pcol")
    place = lax.dynamic_index_in_dim(jnp.array(PLACE_TABLE, jnp.int32), here, 0, keepdims=False)
    sent = pack(place, lhat_parent, lhat_child)
    dealt = [lax.ppermute(value, AXES, pairs) for value, pairs in zip(sent, DEALS)]
    plan, split_tile, *dealt = lax.optimization_barrier(
        (make_plan(place, structure, widths), split_transposed(ancestor_inv), *dealt))
    kept, passed, send_kept, send_passed = lax.switch(
        plan[BUCKET], [products(slots) for slots in CAPACITIES], plan, split_tile, dealt)

    passed = swap_planes(passed + swap_cores(send_passed), True)
    kept = kept + swap_cores(send_kept)
    kept, passed, high, low = lax.optimization_barrier((kept, passed, *turn(plan, lhat_parent, lhat_child)))
    kept = kept + passed
    slab, sums = finish_slab(kept[0], swap_planes(kept[1], False), high, low)

    far_slab = swap_planes(slab, False)
    sums = scatter_sum(sums.reshape(SIDE, -1, LANES), NEAR)
    far_slab, sums = lax.optimization_barrier((far_slab, sums))
    first = jnp.stack([slab, far_slab])
    second, other_first = swap_planes(first, True), swap_cores(first)
    sums = jnp.sum(gather(sums, FAR), axis=0)
    sums = gather(sums, STACK)
    second, other_first, sums = lax.optimization_barrier((second, other_first, sums))
    other_second = swap_cores(second)
    sums = gather(sums, NEAR)
    other_second, sums = lax.optimization_barrier((other_second, sums))
    other_sums = swap_cores(sums)
    inv_sp, inv_sc = finish_rows(plan, (first, second, other_first, other_second), lhat_cross)
    inv_sp, inv_sc, other_sums = lax.optimization_barrier((inv_sp, inv_sc, other_sums))
    inv_pp, inv_pc, inv_cc = finish_blocks(plan, sums, other_sums, lhat_cross, diag_parent, diag_child)
    return (inv_sp, inv_pp, inv_sc, inv_pc, inv_cc)


def solution(mesh):
    return jax.shard_map(
        per_device,
        mesh=mesh,
        in_specs=(P("prow", "pcol"), P("pcol", None), P("pcol", None), P(), P(), P(), P(), P()),
        out_specs=(P("pcol", None), P(), P("pcol", None), P(), P()),
        check_vma=False,
    )
```

```python
import functools

import jax
import jax.numpy as jnp
from jax import lax
from jax.experimental import pallas as pl
from jax.experimental.pallas import tpu as pltpu
from jax.sharding import PartitionSpec as P

BLK = 256
AXES = ("prow", "pcol")
SIDE = 4
LANES = 128
MIB = 1 << 20
SPAN = range(SIDE)
CHUNKS = 2 * SIDE
SLICE = 16
GROUP = SIDE * SLICE
CAPACITIES = (36, 46, 64)
BUCKET, TURNED, PLANE_Z, CORE, OUTER = range(5)
OWN, ROW, WIDTHS, DEST, PLAN_SIZE = 16, 48, 112, 114, 128


def flat(z, k, y, x):
    return ((z % SIDE) * 2 + k) * SIDE * SIDE + (y % SIDE) * SIDE + x % SIDE


PLACES = [(z, k, y, x) for z in SPAN for k in (0, 1) for y in SPAN for x in SPAN]
ROWS_OF_CORE_0 = [[flat(z, 0, y, x) for x in SPAN] for z in SPAN for y in SPAN]
COLS_OF_CORE_0 = [[flat(z, 0, y, x) for y in SPAN] for z in SPAN for x in SPAN]
ROWS_OF_CORE_1 = [[flat(z, 1, y, x) for x in SPAN] for z in SPAN for y in SPAN]
COLS_OF_CORE_1 = [[flat(z, 1, y, x) for y in SPAN] for z in SPAN for x in SPAN]
NEAR = ROWS_OF_CORE_0 + COLS_OF_CORE_1
FAR = COLS_OF_CORE_0 + ROWS_OF_CORE_1
STACK = [[flat(z, k, y, x) for z in SPAN] for k in (0, 1) for y in SPAN for x in SPAN]
STACK = [[flat(z, k, y, x) for z in SPAN] for k in (0, 1) for y in SPAN for x in SPAN]
PLANE = [[flat(z, 0, y, x) for y in SPAN for x in SPAN] for z in SPAN] + [
    [flat(z, 1, y, x) for x in SPAN for y in SPAN] for z in SPAN
]


def piece_of(k, y, x):
    return SIDE * y + x if k == 0 else SIDE * x + y


def deals():
    pairs, slices, turned, used = [[], []], [[0] * 128, [0] * 128], [0] * 128, {}
    for z, k, y, x in PLACES:
        here, p = flat(z, k, y, x), piece_of(k, y, x)
        near = x // 2
        turned[here] = near
        for i, block in enumerate((near, 1 - near)):
            plane = (z + y + 2 * k) % SIDE
            core = used.get((i, z, k, block, plane), 0)
            used[i, z, k, block, plane] = core + 1
            there = flat(plane, core, z, 2 * k + block)
            pairs[i].append((there, here))
            slices[i][there] = p
    rows = [[here // 16, here % 16, slices[0][here], slices[1][here], turned[here]] for here in range(128)]
    return pairs, rows


DEALS, PLACE_TABLE = deals()


def partner(z, k, near):
    return z ^ (1 if (k == 0) == near else 3)


def swap_planes(value, near):
    pairs = [(flat(partner(z, k, near), k, y, x), flat(z, k, y, x)) for z, k, y, x in PLACES]
    return lax.ppermute(value, AXES, pairs)


PLANE_ORDER = ((0, 3, 1, 2), (0, 1, 3, 2))


def plane_at(z, core, place):
    return z ^ jnp.where(core == 0, PLANE_ORDER[0][place], PLANE_ORDER[1][place])


def fetch_far(value, d):
    pairs = [(flat(z, k, y + d * (1 - k), x + d * k), flat(z, k, y, x)) for z, k, y, x in PLACES]
    return lax.ppermute(value, AXES, pairs)


def swap_cores(value):
    pairs = [(flat(z, 1 - k, y, x), flat(z, k, y, x)) for z, k, y, x in PLACES]
    return lax.ppermute(value, AXES, pairs)


def exchange(value, groups):
    return lax.all_to_all(value, AXES, 0, 0, axis_index_groups=groups, tiled=True)


def gather(value, groups):
    size = len(groups[0])
    return exchange(jnp.broadcast_to(value[None], (size,) + value.shape), groups)


def scatter_sum(value, groups):
    return jnp.sum(exchange(value, groups), axis=0)


def split(value):
    high = value.astype(jnp.bfloat16)
    return high, (value - high.astype(jnp.float32)).astype(jnp.bfloat16)


def dot3(left, right, dims=(((1,), (0,)), ((), ()))):
    left_high, left_low = split(left)
    right_high, right_low = split(right)

    def dot(a, b):
        return lax.dot_general(a, b, dims, preferred_element_type=jnp.float32)

    return dot(left_high, right_high) + (dot(left_high, right_low) + dot(left_low, right_high))


def split_transposed_kernel(a_ref, out_ref):
    @pl.loop(0, SIDE)
    def _(o):
        parts = [a_ref[pl.ds(pl.multiple_of(BLK * i + GROUP * o, GROUP), GROUP), :] for i in range(2)]
        high, low = split(jnp.concatenate(parts, axis=0))
        out_ref[0, o, 0] = high.T
        out_ref[0, o, 1] = low.T


def split_transposed(a):
    rows, cols = a.shape
    steps = rows // (2 * BLK)
    out = pl.BlockSpec((1, SIDE, 2, cols, 2 * GROUP), lambda i: (i, 0, 0, 0, 0))
    return pl.pallas_call(
        split_transposed_kernel,
        grid=(steps,),
        in_specs=[pl.BlockSpec((2 * BLK, cols), lambda i: (i, 0))],
        out_specs=out,
        out_shape=jax.ShapeDtypeStruct((steps, SIDE, 2, cols, 2 * GROUP), jnp.bfloat16),
        compiler_params=pltpu.CompilerParams(vmem_limit_bytes=50 * MIB),
        cost_estimate=pl.CostEstimate(flops=rows * cols, bytes_accessed=8 * rows * cols, transcendentals=0),
    )(a)


def smem(*shape):
    return pl.BlockSpec(memory_space=pltpu.SMEM)


def plan_kernel(place_ref, structure_ref, widths_ref, plan_ref, counts):
    r, c = place_ref[0], place_ref[1]
    chunks = [(widths_ref[i] + LANES - 1) // LANES for i in range(2)]

    def count(col, _):
        total = jnp.int32(0)
        for b in range(4):
            for i in range(2):
                total += jnp.where(structure_ref[i, 4 * col + b] > 0, chunks[i], 0)
        counts[col] = total
        return 0

    lax.fori_loop(0, 16, count, 0)
    most_row = lax.fori_loop(0, 8, lambda i, m: jnp.maximum(m, counts[2 * i] + counts[2 * i + 1]), jnp.int32(0))
    bucket = jnp.int32(0)
    for slots in CAPACITIES[:-1]:
        bucket += jnp.where(most_row > slots, 1, 0)
    plan_ref[BUCKET] = bucket

    def mark(start, base, blocks):
        def one(b, run):
            for q in range(CHUNKS):
                active = (structure_ref[q // SIDE, start + b] > 0) & (q % SIDE < chunks[q // SIDE])
                plan_ref[base + b * CHUNKS + q] = jnp.where(active, run, -1)
                run += jnp.where(active, 1, 0)
            return run

        return lax.fori_loop(0, blocks, one, jnp.int32(0))

    mark(4 * c, OWN, 4)
    mark(8 * r, ROW, 8)
    plan_ref[TURNED] = place_ref[4]
    plan_ref[PLANE_Z] = r // 2
    core = lax.rem(r, 2)
    plan_ref[CORE] = core
    plan_ref[OUTER] = jnp.where(core == 0, c // SIDE, lax.rem(c, SIDE))
    for i in range(2):
        plan_ref[WIDTHS + i] = widths_ref[i]
    for q in range(CHUNKS):
        owner = (q % SIDE) // 2
        apart = (r // 2) ^ (2 * (q // SIDE) + q % 2)
        dest = jnp.int32(0)
        for n in range(1, SIDE):
            dest = jnp.where(apart == PLANE_ORDER[owner][n], n, dest)
        plan_ref[DEST + q] = dest + jnp.where(core == owner, 0, SIDE)


def make_plan(place, structure, widths):
    return pl.pallas_call(
        plan_kernel,
        in_specs=[smem()] * 3,
        out_specs=smem(),
        out_shape=jax.ShapeDtypeStruct((PLAN_SIZE,), jnp.int32),
        scratch_shapes=[pltpu.SMEM((16,), jnp.int32)],
    )(place, structure, widths)


def pack_kernel(place_ref, parent_a, parent_b, child_a, child_b, out_a, out_b):
    out_a[0], out_b[0] = parent_a[...], parent_b[...]
    out_a[1], out_b[1] = child_a[...], child_b[...]


def pack(place, parent, child):
    width = parent.shape[1]
    shaped = [panel.reshape(4, BLK, width) for panel in (parent, child)]
    specs = [pl.BlockSpec((4, SLICE, width), lambda i, place, at=at: (0, place[at], 0)) for at in (2, 3)]
    out = pl.BlockSpec((2, 4, SLICE, width), lambda i, place: (0, 0, 0, 0))
    return pl.pallas_call(
        pack_kernel,
        grid_spec=pltpu.PrefetchScalarGridSpec(
            num_scalar_prefetch=1, grid=(1,), in_specs=specs + specs, out_specs=[out, out]
        ),
        out_shape=[jax.ShapeDtypeStruct((2, 4, SLICE, width), jnp.float32)] * 2,
        compiler_params=pltpu.CompilerParams(vmem_limit_bytes=60 * MIB),
        cost_estimate=pl.CostEstimate(flops=0, bytes_accessed=MIB, transcendentals=0),
    )(place, shaped[0], shaped[0], shaped[1], shaped[1])


def merge_kernel(plan_ref, from_a, from_b, out_ref):
    turned = plan_ref[TURNED] > 0

    @pl.loop(0, 4)
    def _(b):
        for q in range(CHUNKS):
            cols = pl.ds(LANES * (q % SIDE), LANES)
            value_a, value_b = from_a[q // SIDE, b, :, cols], from_b[q // SIDE, b, :, cols]
            for half in range(2):
                slot = plan_ref[ROW + (4 * half + b) * CHUNKS + q]
                value = jnp.where(turned == (half == 0), value_b, value_a)

                @pl.when(slot >= 0)
                def _():
                    for i in SPAN:
                        out_ref[i, slot] = value


def merge(plan, from_a, from_b, slots):
    ins = pl.BlockSpec(from_a.shape, lambda i, plan: (0, 0, 0, 0))
    return pl.pallas_call(
        merge_kernel,
        grid_spec=pltpu.PrefetchScalarGridSpec(
            num_scalar_prefetch=1,
            grid=(1,),
            in_specs=[ins, ins],
            out_specs=pl.BlockSpec((SIDE, slots, SLICE, LANES), lambda i, plan: (0, 0, 0, 0)),
        ),
        out_shape=jax.ShapeDtypeStruct((SIDE, slots, SLICE, LANES), jnp.float32),
        compiler_params=pltpu.CompilerParams(vmem_limit_bytes=16 * MIB),
        cost_estimate=pl.CostEstimate(flops=0, bytes_accessed=4 * MIB, transcendentals=0),
    )(plan, from_a, from_b)


def product_kernel(sizes, has_earlier, plan_ref, *refs):
    count = len(sizes)
    tiles, refs = refs[:count], refs[count:]
    pieces, refs = refs[: sum(sizes)], refs[sum(sizes) :]
    out_refs, (panel_high, panel_low) = refs[has_earlier:-2], refs[-2:]
    steps, _, _, tile, lanes = tiles[0].shape
    depth = steps * lanes

    @pl.when(pl.program_id(0) == 0)
    def _():
        @pl.loop(0, depth // GROUP)
        def _(b):
            for q in range(CHUNKS):
                slot = plan_ref[ROW + b * CHUNKS + q]
                lane = lax.broadcasted_iota(jnp.int32, (GROUP, LANES), 1) + LANES * (q % SIDE)
                kept, slot = (lane < plan_ref[WIDTHS + q // SIDE]) & (slot >= 0), jnp.maximum(slot, 0)
                cols = pl.ds(pl.multiple_of(LANES * plan_ref[DEST + q], LANES), LANES)
                first = 0
                for g, size in enumerate(sizes):
                    values = [ref[:, slot].reshape(-1, LANES) for ref in pieces[first : first + size]]
                    first += size
                    value = values[0] if size == 1 else jnp.concatenate(values, axis=0)
                    high, low = split(jnp.where(kept, value, 0.0))
                    rows = pl.ds(pl.multiple_of(GROUP * b + depth * g, GROUP), GROUP)
                    panel_high[rows, cols] = high
                    panel_low[rows, cols] = low

    width = SIDE * LANES

    def half(i):
        cols = pl.ds(width * i, width) if isinstance(i, int) else pl.ds(pl.multiple_of(width * i, width), width)
        total = None
        for g in range(count):
            rows = pl.ds(depth * g, depth)
            both = jnp.concatenate([tiles[g][n, 0].reshape(2 * tile, lanes) for n in range(steps)], axis=1)
            part = jnp.dot(both, panel_high[rows, cols], preferred_element_type=jnp.float32)
            part = part[:tile] + part[tile:]
            part += jnp.dot(both[:tile], panel_low[rows, cols], preferred_element_type=jnp.float32)
            total = part if total is None else total + part
        return [total[:, LANES * q : LANES * (q + 1)] for q in SPAN]

    if len(out_refs) == 1:

        @pl.loop(0, 2)
        def _(i):
            for q, value in enumerate(half(i)):
                out_refs[0][SIDE * i + q] = value + refs[0][SIDE * i + q] if has_earlier else value
    else:
        for i in range(2):
            for q, value in enumerate(half(i)):
                out_refs[2 * i + q // 2][q % 2] = value + refs[0][SIDE * i + q]


def product(plan, split_tile, shifts, groups, earlier=None, is_last=False):
    steps, _, _, cols, lanes = split_tile.shape
    depth = steps * lanes
    tile = 256
    pieces = [piece for group in groups for piece in group]
    whole = pl.BlockSpec((CHUNKS, tile, LANES), lambda i, plan: (0, i, 0))
    pair = pl.BlockSpec((2, tile, LANES), lambda i, plan: (0, i, 0))
    tiles = [
        pl.BlockSpec(
            (steps, 1, 2, tile, lanes), lambda i, plan, shift=shift: (0, lax.rem(plan[OUTER] + shift, SIDE), 0, i, 0))
        for shift in shifts
    ]
    kernel = functools.partial(product_kernel, [len(group) for group in groups], earlier is not None)
    return pl.pallas_call(
        kernel,
        grid_spec=pltpu.PrefetchScalarGridSpec(
            num_scalar_prefetch=1,
            grid=(cols // tile,),
            in_specs=tiles
            + [pl.BlockSpec(piece.shape, lambda i, plan: (0, 0, 0, 0)) for piece in pieces]
            + [whole] * (earlier is not None),
            out_specs=[pair] * 4 if is_last else whole,
            scratch_shapes=[pltpu.VMEM((depth * len(shifts), CHUNKS * LANES), jnp.bfloat16)] * 2,
        ),
        out_shape=[jax.ShapeDtypeStruct((2, cols, LANES), jnp.float32)] * 4
        if is_last
        else jax.ShapeDtypeStruct((CHUNKS, cols, LANES), jnp.float32),
        compiler_params=pltpu.CompilerParams(vmem_limit_bytes=32 * MIB),
        cost_estimate=pl.CostEstimate(
            flops=6 * len(shifts) * depth * cols * CHUNKS * LANES, bytes_accessed=12 * MIB, transcendentals=0
        ),
    )(plan, *[split_tile] * len(shifts), *pieces, *([] if earlier is None else [earlier]))


def products(slots):
    def run(plan, split_tile, dealt):
        near = exchange(merge(plan, *dealt, slots), NEAR)
        ahead, behind = fetch_far(near, 1), fetch_far(near, 3)
        total = product(plan, split_tile, (0,), ((near,),))
        total, ahead, behind = lax.optimization_barrier((total, ahead, behind))
        far_first, far_last = fetch_far(ahead[:2], 1), fetch_far(behind[2:], 3)
        total = product(plan, split_tile, (1, 3), ((ahead,), (behind,)), total)
        return product(plan, split_tile, (2,), ((far_first, far_last),), total, True)

    return run


def turn_kernel(plan_ref, parent_ref, child_ref, high_ref, low_ref):
    first = slab_chunk(plan_ref[PLANE_Z], plan_ref[CORE])
    t = pl.program_id(0)
    q = lax.rem(first + t, CHUNKS)
    lane = lax.broadcasted_iota(jnp.int32, (BLK, LANES), 1)
    for panel, ref in enumerate((parent_ref, child_ref)):

        @pl.when(q // SIDE == panel)
        def _():
            start = LANES * lax.rem(q, SIDE)
            cols = pl.ds(pl.multiple_of(start, LANES), LANES)
            mask = jnp.where(lane + start < plan_ref[WIDTHS + panel], 1.0, 0.0)
            for b in range(4):
                keep = jnp.where(plan_ref[OWN + b * CHUNKS + SIDE * panel] >= 0, 1.0, 0.0)
                rows = pl.ds(BLK * b, BLK)
                high, low = split(ref[rows, cols] * mask * keep)
                high_ref[:, rows] = high.T
                low_ref[:, rows] = low.T


def turn(plan, parent, child):
    rows, width = parent.shape
    out = pl.BlockSpec((LANES, rows), lambda t, plan: (t, 0))
    panel = pl.BlockSpec((rows, width), lambda t, plan: (0, 0))
    return pl.pallas_call(
        turn_kernel,
        grid_spec=pltpu.PrefetchScalarGridSpec(
            num_scalar_prefetch=1, grid=(5,), in_specs=[panel, panel], out_specs=[out, out]
        ),
        out_shape=[jax.ShapeDtypeStruct((5 * LANES, rows), jnp.bfloat16)] * 2,
        compiler_params=pltpu.CompilerParams(vmem_limit_bytes=48 * MIB),
        cost_estimate=pl.CostEstimate(flops=MIB, bytes_accessed=8 * MIB, transcendentals=0),
    )(plan, parent, child)


def slab_kernel(kept_ref, passed_ref, high_ref, low_ref, slab_ref, sums_ref):
    slab = kept_ref[...] + passed_ref[...]
    slab_ref[...] = slab
    slab_high, slab_low = split(slab)
    total = jnp.dot(high_ref[...], slab_high, preferred_element_type=jnp.float32)
    total += jnp.dot(high_ref[...], slab_low, preferred_element_type=jnp.float32)
    sums_ref[...] = total + jnp.dot(low_ref[...], slab_high, preferred_element_type=jnp.float32)


def finish_slab(kept, passed, high, low):
    rows, width = kept.shape
    return pl.pallas_call(
        slab_kernel,
        out_shape=[
            jax.ShapeDtypeStruct((rows, width), jnp.float32),
            jax.ShapeDtypeStruct((high.shape[0], width), jnp.float32),
        ],
        compiler_params=pltpu.CompilerParams(vmem_limit_bytes=16 * MIB),
        cost_estimate=pl.CostEstimate(flops=6 * high.size * width, bytes_accessed=6 * MIB, transcendentals=0),
    )(kept, passed, high, low)


def slab_chunk(z, k):
    return SIDE * (z // 2) + 2 * k + lax.rem(z, 2)


def masked_cross(plan_ref, cross_ref):
    rows = lax.broadcasted_iota(jnp.int32, cross_ref.shape, 0)
    cols = lax.broadcasted_iota(jnp.int32, cross_ref.shape, 1)
    keep = jnp.where(rows < plan_ref[WIDTHS], 1.0, 0.0) * jnp.where(cols < plan_ref[WIDTHS + 1], 1.0, 0.0)
    return cross_ref[...] * keep


def masked_square(ref, width):
    rows = lax.broadcasted_iota(jnp.int32, ref.shape, 0)
    cols = lax.broadcasted_iota(jnp.int32, ref.shape, 1)
    return ref[...] * (jnp.where(rows < width, 1.0, 0.0) * jnp.where(cols < width, 1.0, 0.0))


def rows_kernel(plan_ref, own_a, own_b, other_a, other_b, cross_ref, inv_sp_ref, inv_sc_ref, total):
    z, k = plan_ref[PLANE_Z], plan_ref[CORE]
    for refs, core in (((own_a, own_b), k), ((other_a, other_b), 1 - k)):
        for i in SPAN:
            start = LANES * slab_chunk(plane_at(z, core, i), core)
            total[:, pl.ds(pl.multiple_of(start, LANES), LANES)] = refs[i // 2][i % 2]
    width = cross_ref.shape[0]
    block = OWN + pl.program_id(0) * CHUNKS
    keep = [jnp.where(plan_ref[block + SIDE * i] >= 0, 1.0, 0.0) for i in range(2)]
    inv_sp = -total[:, :width] * keep[0]
    inv_sp_ref[...] = inv_sp
    inv_sc_ref[...] = -(total[:, width:] + dot3(inv_sp, masked_cross(plan_ref, cross_ref))) * keep[1]


def finish_rows(plan, slabs, cross):
    _, rows, _ = slabs[0].shape
    width = cross.shape[0]
    pair = pl.BlockSpec((2, BLK, LANES), lambda i, plan: (0, i, 0))
    whole = pl.BlockSpec((BLK, width), lambda i, plan: (i, 0))
    return pl.pallas_call(
        rows_kernel,
        grid_spec=pltpu.PrefetchScalarGridSpec(
            num_scalar_prefetch=1,
            grid=(rows // BLK,),
            in_specs=[pair] * 4 + [pl.BlockSpec((width, width), lambda i, plan: (0, 0))],
            out_specs=[whole, whole],
            scratch_shapes=[pltpu.VMEM((BLK, 2 * width), jnp.float32)],
        ),
        out_shape=[jax.ShapeDtypeStruct((rows, width), jnp.float32)] * 2,
        compiler_params=pltpu.CompilerParams(vmem_limit_bytes=32 * MIB),
        cost_estimate=pl.CostEstimate(flops=6 * rows * width * width, bytes_accessed=16 * rows * width, transcendentals=0),
    )(plan, *slabs, cross)


def blocks_kernel(
    plan_ref, own_ref, other_ref, cross_ref, parent_ref, child_ref, inv_pp_ref, inv_pc_ref, inv_cc_ref, slab, total
):
    share = own_ref.shape[2]
    k = plan_ref[CORE]
    for ref, core in ((own_ref, k), (other_ref, 1 - k)):
        for z in SPAN:
            j = SIDE * (z // 2) + 2 * core + z % 2
            for i in SPAN:
                slab[j, pl.ds(share * i, share), :] = ref[i, z]
    for j in range(CHUNKS):
        for i in range(CHUNKS):
            t = (i - j) % CHUNKS
            if t <= 4:
                block = slab[j, pl.ds(LANES * t, LANES), :]
            else:
                block = slab[i, pl.ds(LANES * (CHUNKS - t), LANES), :].T
            total[pl.ds(LANES * i, LANES), pl.ds(LANES * j, LANES)] = block
    width = cross_ref.shape[0]
    cross = masked_cross(plan_ref, cross_ref)
    inv_pp = masked_square(parent_ref, plan_ref[WIDTHS]) + total[:width, :width]
    inv_pp_ref[...] = inv_pp
    inv_pc = total[:width, width:] - dot3(inv_pp, cross)
    inv_pc_ref[...] = inv_pc
    last = dot3(cross, inv_pc, (((0,), (0,)), ((), ()))) + dot3(total[width:, :width], cross)
    inv_cc_ref[...] = masked_square(child_ref, plan_ref[WIDTHS + 1]) + total[width:, width:] - last


def finish_blocks(plan, own, other, cross, parent, child):
    width = cross.shape[0]
    square = pl.BlockSpec((width, width), lambda i, plan: (0, 0))
    sums = pl.BlockSpec(own.shape, lambda i, plan: (0, 0, 0, 0))
    return pl.pallas_call(
        blocks_kernel,
        grid_spec=pltpu.PrefetchScalarGridSpec(
            num_scalar_prefetch=1,
            grid=(1,),
            in_specs=[sums, sums] + [square] * 3,
            out_specs=[square] * 3,
            scratch_shapes=[
                pltpu.VMEM((CHUNKS, 5 * LANES, LANES), jnp.float32),
                pltpu.VMEM((2 * width, 2 * width), jnp.float32),
            ],
        ),
        out_shape=[jax.ShapeDtypeStruct((width, width), jnp.float32)] * 3,
        compiler_params=pltpu.CompilerParams(vmem_limit_bytes=32 * MIB),
        cost_estimate=pl.CostEstimate(flops=18 * width**3, bytes_accessed=40 * width * width, transcendentals=0),
    )(plan, own, other, cross, parent, child)


def per_device(
    ancestor_inv, lhat_parent, lhat_child, lhat_cross, diag_parent, diag_child, structure, widths
):
    here = lax.axis_index("prow") * 16 + lax.axis_index("pcol")
    place = lax.dynamic_index_in_dim(jnp.array(PLACE_TABLE, jnp.int32), here, 0, keepdims=False)
    sent = pack(place, lhat_parent, lhat_child)
    dealt = [lax.ppermute(value, AXES, pairs) for value, pairs in zip(sent, DEALS)]
    plan, split_tile, *dealt = lax.optimization_barrier(
        (make_plan(place, structure, widths), split_transposed(ancestor_inv), *dealt))
    kept, passed, send_kept, send_passed = lax.switch(
        plan[BUCKET], [products(slots) for slots in CAPACITIES], plan, split_tile, dealt)

    passed = swap_planes(passed + swap_cores(send_passed), True)
    kept = kept + swap_cores(send_kept)
    kept, passed, high, low = lax.optimization_barrier((kept, passed, *turn(plan, lhat_parent, lhat_child)))
    kept = kept + passed
    slab, sums = finish_slab(kept[0], swap_planes(kept[1], False), high, low)

    far_slab = swap_planes(slab, False)
    sums = scatter_sum(sums.reshape(SIDE, -1, LANES), NEAR)
    far_slab, sums = lax.optimization_barrier((far_slab, sums))
    first = jnp.stack([slab, far_slab])
    second, other_first = swap_planes(first, True), swap_cores(first)
    sums = jnp.sum(gather(sums, FAR), axis=0)
    sums = gather(sums, STACK)
    second, other_first, sums = lax.optimization_barrier((second, other_first, sums))
    other_second = swap_cores(second)
    sums = gather(sums, NEAR)
    other_second, sums = lax.optimization_barrier((other_second, sums))
    other_sums = swap_cores(sums)
    inv_sp, inv_sc = finish_rows(plan, (first, second, other_first, other_second), lhat_cross)
    inv_sp, inv_sc, other_sums = lax.optimization_barrier((inv_sp, inv_sc, other_sums))
    inv_pp, inv_pc, inv_cc = finish_blocks(plan, sums, other_sums, lhat_cross, diag_parent, diag_child)
    return (inv_sp, inv_pp, inv_sc, inv_pc, inv_cc)


def solution(mesh):
    return jax.shard_map(
        per_device,
        mesh=mesh,
        in_specs=(P("prow", "pcol"), P("pcol", None), P("pcol", None), P(), P(), P(), P(), P()),
        out_specs=(P("pcol", None), P(), P("pcol", None), P(), P()),
        check_vma=False,
    )
```
